32 devices in a mesh: dp: 4 (over y, x), mp: 8 (over z, core).
Axes of the slice: x: 2, y: 2, z: 4, core: 2. Of those that a mesh axis runs over, the one named last changes fastest.
Arguments:
- frames: bfloat16 [8, 1664, 1024], P('dp', 'mp'), may hold values from -6 to 6
- lengths: int32 [8], P('dp'), may hold values from 554 to 1664
- mask_flags: int32 [8, 1664], P('dp', 'mp'), may hold values from 0 to 1, as said below
- mask_embed: float32 [1024], replicated, may hold values from -6 to 6
- ffa_gain: float32 [1024], replicated, may hold values from 0.1 to 1.9
- ffa_shift: float32 [1024], replicated, may hold values from -3 to 3
- ffa_w_in: bfloat16 [1024, 4096], P(None, 'mp'), may hold values from -0.1875 to 0.1875
- ffa_b_in: bfloat16 [4096], P('mp'), may hold values from -3 to 3
- ffa_w_out: bfloat16 [4096, 1024], P('mp'), may hold values from -0.1875 to 0.1875
- ffa_b_out: float32 [1024], replicated, may hold values from -3 to 3
- att_gain: float32 [1024], replicated, may hold values from 0.1 to 1.9
- att_shift: float32 [1024], replicated, may hold values from -3 to 3
- att_w_qkv: bfloat16 [3, 1024, 1024], P(None, None, 'mp'), may hold values from -0.1875 to 0.1875
- att_b_qv: float32 [2, 1024], P(None, 'mp'), may hold values from -2.5 to 2.5
- att_w_out: bfloat16 [1024, 1024], P('mp'), may hold values from -1.5 to 1.5
- att_b_out: float32 [1024], replicated, may hold values from -3 to 3
- conv_gain: float32 [1024], replicated, may hold values from 0.1 to 1.9
- conv_shift: float32 [1024], replicated, may hold values from -3 to 3
- conv_w_in: bfloat16 [2, 1024, 1024], P(None, None, 'mp'), may hold values from -0.1875 to 0.1875
- conv_b_in: float32 [2, 1024], P(None, 'mp'), may hold values from -3 to 3
- conv_w_depth: float32 [31, 1024], P(None, 'mp'), may hold values from -1 to 1
- batch_scale: float32 [1024], P('mp'), may hold values from 0.1 to 1.9
- batch_shift: float32 [1024], P('mp'), may hold values from -3 to 3
- running_mean: float32 [1024], P('mp'), may hold values from -3 to 3
- running_var: float32 [1024], P('mp'), may hold values from 0.02 to 0.25
- conv_w_out: bfloat16 [1024, 1024], P('mp'), may hold values from -0.1875 to 0.1875
- conv_b_out: float32 [1024], replicated, may hold values from -3 to 3
- ffb_gain: float32 [1024], replicated, may hold values from 0.1 to 1.9
- ffb_shift: float32 [1024], replicated, may hold values from -3 to 3
- ffb_w_in: bfloat16 [1024, 4096], P(None, 'mp'), may hold values from -0.1875 to 0.1875
- ffb_b_in: bfloat16 [4096], P('mp'), may hold values from -3 to 3
- ffb_w_out: bfloat16 [4096, 1024], P('mp'), may hold values from -0.1875 to 0.1875
- ffb_b_out: float32 [1024], replicated, may hold values from -3 to 3
- final_gain: float32 [1024], replicated, may hold values from 0.1 to 1.9
- final_shift: float32 [1024], replicated, may hold values from -3 to 3
- cotangent: bfloat16 [8, 1664, 1024], P('dp', 'mp'), may hold values from -6 to 6
Outputs:
- layer_out: float32 [8, 1664, 1024], P('dp', 'mp')
- grad_frames: float32 [8, 1664, 1024], P('dp', 'mp')
- grad_mask_embed: float32 [1024], replicated
- grad_ffa_gain: float32 [1024], replicated
- grad_ffa_shift: float32 [1024], replicated
- grad_ffa_w_in: float32 [1024, 4096], P(None, 'mp')
- grad_ffa_b_in: float32 [4096], P('mp')
- grad_ffa_w_out: float32 [4096, 1024], P('mp')
- grad_ffa_b_out: float32 [1024], replicated
- grad_att_gain: float32 [1024], replicated
- grad_att_shift: float32 [1024], replicated
- grad_att_w_qkv: float32 [3, 1024, 1024], P(None, None, 'mp')
- grad_att_b_qv: float32 [2, 1024], P(None, 'mp')
- grad_att_w_out: float32 [1024, 1024], P('mp')
- grad_att_b_out: float32 [1024], replicated
- grad_conv_gain: float32 [1024], replicated
- grad_conv_shift: float32 [1024], replicated
- grad_conv_w_in: float32 [2, 1024, 1024], P(None, None, 'mp')
- grad_conv_b_in: float32 [2, 1024], P(None, 'mp')
- grad_conv_w_depth: float32 [31, 1024], P(None, 'mp')
- grad_batch_scale: float32 [1024], P('mp')
- grad_batch_shift: float32 [1024], P('mp')
- grad_conv_w_out: float32 [1024, 1024], P('mp')
- grad_conv_b_out: float32 [1024], replicated
- grad_ffb_gain: float32 [1024], replicated
- grad_ffb_shift: float32 [1024], replicated
- grad_ffb_w_in: float32 [1024, 4096], P(None, 'mp')
- grad_ffb_b_in: float32 [4096], P('mp')
- grad_ffb_w_out: float32 [4096, 1024], P('mp')
- grad_ffb_b_out: float32 [1024], replicated
- grad_final_gain: float32 [1024], replicated
- grad_final_shift: float32 [1024], replicated
- new_mean: float32 [1024], P('mp')
- new_var: float32 [1024], P('mp')
The draws below stay inside these ranges and needn't reach their ends.
Inputs may be any that keep to these rules, and one draw needn't show every extreme that they name: `mask_flags`: only frames below the item's length are marked.
All inputs are finite; a program needn't handle non-finite values.
Results may differ from the reference program's by a relative error of at most 0.017.
The reference program's roundings to bfloat16 on the way count: a program that leaves them out, or rounds other values in their place, can miss the bound.
Values may be sent and summed in bfloat16 or wider, within the bound.
No kernel may reach another device: no remote copies, remote signals or barrier semaphores. Data moves between devices by JAX's collectives and lax.ppermute only.
A program may use at most 256 MiB of HBM per device.

```python
import math
import jax
import jax.numpy as jnp
from jax import lax

D = 1024
HEADS = 16
HEAD = 64
FF = 4096
KERNEL = 31
L = 1664
ITEMS = 8


def item_lengths(key):
    item_index = jnp.arange(ITEMS)
    least_len = L // 3
    rising = least_len + (L - least_len) * item_index // max(ITEMS - 1, 1)
    jitter = jax.random.randint(jax.random.fold_in(key, 11), (ITEMS,), 0, L // 8 + 1)
    drawn_lengths = jnp.maximum(rising - jitter, least_len)
    return jnp.where(item_index == ITEMS - 1, L, drawn_lengths).astype(jnp.int32)


def draw_lengths(key, part):
    return item_lengths(key)


def draw_mask_flags(key, part):
    drawn_lengths = item_lengths(key)
    halvings = jax.random.randint(jax.random.fold_in(key, 12), (ITEMS,), 0, 7)
    masked_count = jnp.maximum(drawn_lengths // jnp.left_shift(jnp.ones_like(halvings), halvings), 1)
    item_keys = jax.random.split(jax.random.fold_in(key, 13), ITEMS)
    priority = jax.vmap(lambda item_key: jax.random.permutation(item_key, L))(item_keys)
    frame_index = jnp.arange(L)[None, :]
    chosen = (priority * drawn_lengths[:, None] < masked_count[:, None] * L) & (frame_index < drawn_lengths[:, None])
    return chosen.astype(jnp.int32)


def block_scale(rng, extent, pieces, smallest, top_value):
    factor_of = 1.0
    for dim, shards_of in pieces:
        draws = jax.random.uniform(jax.random.fold_in(jax.random.fold_in(rng, 6), dim), (shards_of,), jnp.float32, smallest / len(pieces), top_value / len(pieces))
        factor_of = factor_of * jnp.repeat(jnp.exp(draws), extent[dim] // shards_of).reshape((-1,) + (1,) * (len(extent) - 1 - dim))
    return factor_of


def noise(stream_key, shape, deviation, bound, cuts=(), held_as=jnp.bfloat16):
    result = deviation * jax.random.normal(stream_key, shape, jnp.float32)
    if cuts:
        result = result * block_scale(stream_key, shape, cuts, -0.22, 0.18)
    return jnp.clip(result, -bound, bound).astype(held_as)


def setup_inputs(seed: int = 0) -> dict:
    key_of = jax.random.split(jax.random.key(seed), 37)
    frames = noise(key_of[0], (ITEMS, L, D), 1.0, 6.0, ((0, 4), (1, 8)))
    lengths = draw_lengths(jax.random.fold_in(key_of[36], 71), 0)
    mask_flags = draw_mask_flags(jax.random.fold_in(key_of[36], 71), 0)
    mask_embed = noise(key_of[3], (D,), 1.0, 6.0, (), jnp.float32)
    ffa_gain = jnp.clip(1.0 + 0.18 * jax.random.normal(key_of[4], (D,), jnp.float32), 0.1, 1.9)
    ffa_shift = noise(key_of[5], (D,), 0.5, 3.0, (), jnp.float32)
    ffa_w_in = noise(key_of[6], (D, FF), D ** -0.5, 0.1875, ((1, 8),))
    ffa_b_in = noise(key_of[7], (FF,), 0.5, 3.0, ((0, 8),))
    ffa_w_out = noise(key_of[8], (FF, D), (FF // 4) ** -0.5, 0.1875, ((0, 8),))
    ffa_b_out = noise(key_of[9], (D,), 0.5, 3.0, (), jnp.float32)
    att_gain = jnp.clip(1.0 + 0.18 * jax.random.normal(key_of[10], (D,), jnp.float32), 0.1, 1.9)
    att_shift = noise(key_of[11], (D,), 0.5, 3.0, (), jnp.float32)
    att_w_qkv = noise(key_of[12], (3, D, D), D ** -0.5, 0.1875, ((2, 8),))
    att_b_qv = noise(key_of[13], (2, D), 0.4, 2.5, ((1, 8),), jnp.float32)
    att_w_out = noise(key_of[14], (D, D), (D // 64) ** -0.5, 1.5, ((0, 8),))
    att_b_out = noise(key_of[15], (D,), 0.5, 3.0, (), jnp.float32)
    conv_gain = jnp.clip(1.0 + 0.18 * jax.random.normal(key_of[16], (D,), jnp.float32), 0.1, 1.9)
    conv_shift = noise(key_of[17], (D,), 0.5, 3.0, (), jnp.float32)
    conv_w_in = noise(key_of[18], (2, D, D), D ** -0.5, 0.1875, ((2, 8),))
    conv_b_in = noise(key_of[19], (2, D), 0.5, 3.0, ((1, 8),), jnp.float32)
    conv_w_depth = noise(key_of[20], (KERNEL, D), KERNEL ** -0.5, 1.0, ((1, 8),), jnp.float32)
    batch_scale = jnp.clip(1.0 + 0.18 * jax.random.normal(key_of[21], (D,), jnp.float32), 0.1, 1.9)
    batch_shift = noise(key_of[22], (D,), 0.5, 3.0, ((0, 8),), jnp.float32)
    running_mean = noise(key_of[23], (D,), 0.5, 3.0, ((0, 8),), jnp.float32)
    running_var = jnp.clip(jnp.exp(math.log(0.25) - 2.5257287 * jax.random.uniform(key_of[24], (D,), jnp.float32) ** block_scale(key_of[24], (D,), ((0, 8),), -0.2, 0.2)), 0.02, 0.25)
    conv_w_out = noise(key_of[25], (D, D), D ** -0.5, 0.1875, ((0, 8),))
    conv_b_out = noise(key_of[26], (D,), 0.5, 3.0, (), jnp.float32)
    ffb_gain = jnp.clip(1.0 + 0.18 * jax.random.normal(key_of[27], (D,), jnp.float32), 0.1, 1.9)
    ffb_shift = noise(key_of[28], (D,), 0.5, 3.0, (), jnp.float32)
    ffb_w_in = noise(key_of[29], (D, FF), D ** -0.5, 0.1875, ((1, 8),))
    ffb_b_in = noise(key_of[30], (FF,), 0.5, 3.0, ((0, 8),))
    ffb_w_out = noise(key_of[31], (FF, D), (FF // 4) ** -0.5, 0.1875, ((0, 8),))
    ffb_b_out = noise(key_of[32], (D,), 0.5, 3.0, (), jnp.float32)
    final_gain = jnp.clip(1.0 + 0.18 * jax.random.normal(key_of[33], (D,), jnp.float32), 0.1, 1.9)
    final_shift = noise(key_of[34], (D,), 0.5, 3.0, (), jnp.float32)
    cotangent = noise(key_of[35], (ITEMS, L, D), 1.0, 6.0, ((0, 4), (1, 8)))
    return {"frames": frames, "lengths": lengths, "mask_flags": mask_flags, "mask_embed": mask_embed, "ffa_gain": ffa_gain, "ffa_shift": ffa_shift, "ffa_w_in": ffa_w_in, "ffa_b_in": ffa_b_in, "ffa_w_out": ffa_w_out, "ffa_b_out": ffa_b_out, "att_gain": att_gain, "att_shift": att_shift, "att_w_qkv": att_w_qkv, "att_b_qv": att_b_qv, "att_w_out": att_w_out, "att_b_out": att_b_out, "conv_gain": conv_gain, "conv_shift": conv_shift, "conv_w_in": conv_w_in, "conv_b_in": conv_b_in, "conv_w_depth": conv_w_depth, "batch_scale": batch_scale, "batch_shift": batch_shift, "running_mean": running_mean, "running_var": running_var, "conv_w_out": conv_w_out, "conv_b_out": conv_b_out, "ffb_gain": ffb_gain, "ffb_shift": ffb_shift, "ffb_w_in": ffb_w_in, "ffb_b_in": ffb_b_in, "ffb_w_out": ffb_w_out, "ffb_b_out": ffb_b_out, "final_gain": final_gain, "final_shift": final_shift, "cotangent": cotangent}


EPS = 1e-05
HIGHEST = lax.Precision.HIGHEST

@jax.custom_vjp
def low(v):
    return lax.optimization_barrier(v.astype(jnp.bfloat16)).astype(jnp.float32)

@jax.custom_vjp
def low_back(v):
    return v

def low_keep(v):
    return (low(v), None)

def low_pass(kept, grad):
    return (grad,)

def back_keep(v):
    return (v, None)

def back_low(kept, grad):
    return (low(grad),)
low.defvjp(low_keep, low_pass)
low_back.defvjp(back_keep, back_low)

def layer_norm(values, gain_vec, shift_vec):
    row_mean = lax.optimization_barrier(jnp.mean(values, axis=-1, keepdims=True))
    centred = values - row_mean
    row_var = lax.optimization_barrier(jnp.mean(centred * centred, axis=-1, keepdims=True))
    return centred * lax.rsqrt(row_var + EPS) * gain_vec + shift_vec

def project(values, weight):
    return jnp.einsum('ild,dc->ilc', values, weight, precision=HIGHEST)

def feed_forward(hidden_in, gain_vec, shift_vec, w_in, b_in, w_out, b_out):
    act_rows = low(layer_norm(hidden_in, gain_vec, shift_vec))
    upper_rows = low_back(project(act_rows, w_in) + b_in)
    swished = low(jax.nn.silu(upper_rows))
    return low_back(project(swished, w_out) + b_out)

def attend_item(query_rows, key_rows, value_rows, length):
    frame_count = query_rows.shape[0]
    query_heads = query_rows.reshape(frame_count, HEADS, HEAD)
    key_heads = key_rows.reshape(frame_count, HEADS, HEAD)
    value_heads = value_rows.reshape(frame_count, HEADS, HEAD)
    scores = low_back(jnp.einsum('qhe,khe->hqk', query_heads, key_heads, precision=HIGHEST) * (1.0 / math.sqrt(HEAD)))
    visible = jnp.arange(frame_count) < length
    scores = jnp.where(visible[None, None, :], scores, -1e+30)
    attn_probs = low(jax.nn.softmax(scores, axis=-1))
    mixed_rows = jnp.einsum('hqk,khe->qhe', attn_probs, value_heads, precision=HIGHEST)
    return mixed_rows.reshape(frame_count, HEADS * HEAD)

def attention(hidden_in, lengths, gain_vec, shift_vec, w_qkv, b_qv, w_out, b_out):
    act_rows = low(layer_norm(hidden_in, gain_vec, shift_vec))
    stacked = jnp.einsum('ild,kdc->kilc', act_rows, w_qkv, precision=HIGHEST)
    query_rows = low_back(low(stacked[0] + b_qv[0]))
    key_rows = low_back(low(stacked[1]))
    value_rows = low_back(low(stacked[2] + b_qv[1]))
    per_item = jax.checkpoint(lambda packed: attend_item(packed[0], packed[1], packed[2], packed[3]))
    mixed_rows = lax.map(per_item, (query_rows, key_rows, value_rows, lengths))
    mixed_rows = low_back(low(mixed_rows))
    return low_back(project(mixed_rows, w_out) + b_out)

def depthwise(signal, kernel):
    half_width = kernel.shape[0] // 2
    frame_count = signal.shape[1]
    padded = jnp.pad(signal, ((0, 0), (half_width, half_width), (0, 0)))
    summed = jnp.zeros_like(signal)
    for offset in range(kernel.shape[0]):
        summed = summed + padded[:, offset:offset + frame_count, :] * kernel[offset]
    return summed

def convolve(hidden_in, visible, gain_vec, shift_vec, w_in, b_in, w_depth, bn_scale, bn_shift, w_out, b_out):
    act_rows = low(layer_norm(hidden_in, gain_vec, shift_vec))
    both_halves = low_back(jnp.einsum('ild,kdc->kilc', act_rows, w_in, precision=HIGHEST) + b_in[:, None, None, :])
    gated_rows = both_halves[0] * jax.nn.sigmoid(both_halves[1]) * visible[..., None]
    depth_out = depthwise(gated_rows, w_depth)
    valid_count = jnp.sum(visible)
    batch_mean = lax.optimization_barrier(jnp.sum(depth_out * visible[..., None], axis=(0, 1))) / valid_count
    centred = depth_out - batch_mean
    batch_var = lax.optimization_barrier(jnp.sum(centred * centred * visible[..., None], axis=(0, 1))) / valid_count
    normed = centred * lax.rsqrt(batch_var + EPS) * bn_scale + bn_shift
    swished = low(jax.nn.silu(normed))
    return (low_back(project(swished, w_out) + b_out), (batch_mean, batch_var, valid_count))

def reference(frames, lengths, mask_flags, mask_embed, ffa_gain, ffa_shift, ffa_w_in, ffa_b_in, ffa_w_out, ffa_b_out, att_gain, att_shift, att_w_qkv, att_b_qv, att_w_out, att_b_out, conv_gain, conv_shift, conv_w_in, conv_b_in, conv_w_depth, batch_scale, batch_shift, running_mean, running_var, conv_w_out, conv_b_out, ffb_gain, ffb_shift, ffb_w_in, ffb_b_in, ffb_w_out, ffb_b_out, final_gain, final_shift, cotangent):

    def to_wide(member):
        return member.astype(jnp.float32)
    ffa_params = tuple((to_wide(member) for member in (ffa_gain, ffa_shift, ffa_w_in, ffa_b_in, ffa_w_out, ffa_b_out)))
    att_params = tuple((to_wide(member) for member in (att_gain, att_shift, att_w_qkv, att_b_qv, att_w_out, att_b_out)))
    conv_params = tuple((to_wide(member) for member in (conv_gain, conv_shift, conv_w_in, conv_b_in, conv_w_depth, batch_scale, batch_shift, conv_w_out, conv_b_out)))
    ffb_params = tuple((to_wide(member) for member in (ffb_gain, ffb_shift, ffb_w_in, ffb_b_in, ffb_w_out, ffb_b_out)))
    final_params = (to_wide(final_gain), to_wide(final_shift))
    visible = (jnp.arange(L)[None, :] < lengths[:, None]).astype(jnp.float32)
    flag_rows = mask_flags.astype(jnp.float32)

    def forward(frames_in, embed_vec, ffa_p, att_p, conv_p, ffb_p, final_p):
        resid = frames_in + flag_rows[..., None] * embed_vec
        resid = resid + 0.5 * feed_forward(resid, *ffa_p)
        resid = resid + attention(resid, lengths, *att_p)
        branch, batch_stats = convolve(resid, visible, *conv_p)
        resid = resid + branch
        resid = resid + 0.5 * feed_forward(resid, *ffb_p)
        return (layer_norm(resid, *final_p), batch_stats)
    layer_out, pullback, batch_stats = jax.vjp(forward, to_wide(frames), to_wide(mask_embed), ffa_params, att_params, conv_params, ffb_params, final_params, has_aux=True)
    all_grads = pullback(to_wide(cotangent))
    grad_frames, grad_embed, grad_ffa, grad_att, grad_conv, grad_ffb, grad_final = all_grads
    batch_mean, batch_var, valid_count = batch_stats
    new_mean = 0.9 * running_mean + 0.1 * batch_mean
    new_var = 0.9 * running_var + 0.1 * batch_var * valid_count / (valid_count - 1.0)
    return (layer_out, grad_frames, grad_embed, grad_ffa[0], grad_ffa[1], grad_ffa[2], grad_ffa[3], grad_ffa[4], grad_ffa[5], grad_att[0], grad_att[1], grad_att[2], grad_att[3], grad_att[4], grad_att[5], grad_conv[0], grad_conv[1], grad_conv[2], grad_conv[3], grad_conv[4], grad_conv[5], grad_conv[6], grad_conv[7], grad_conv[8], grad_ffb[0], grad_ffb[1], grad_ffb[2], grad_ffb[3], grad_ffb[4], grad_ffb[5], grad_final[0], grad_final[1], new_mean, new_var)
```

```python
import functools
import math

import jax
import jax.numpy as jnp
from jax import lax
from jax.experimental import pallas as pl
from jax.experimental.pallas import tpu as pltpu
from jax.sharding import PartitionSpec as P

HEAD = 64
EPS = 1e-05
BF = jnp.bfloat16
F32 = jnp.float32
LOG2E = math.log2(math.e)


def dot_nn(left, right):
    return lax.dot_general(left, right, (((1,), (0,)), ((), ())), preferred_element_type=F32)


def dot_nt(left, right):
    return lax.dot_general(left, right, (((1,), (1,)), ((), ())), preferred_element_type=F32)


def dot_tn(left, right):
    return lax.dot_general(left, right, (((0,), (0,)), ((), ())), preferred_element_type=F32)


def swap(values, axis, bit):
    count = lax.axis_size(axis)
    return lax.ppermute(values, axis, [(i, i ^ bit) for i in range(count)])


def bits_of(count):
    return [1 << k for k in range(count.bit_length() - 1)]


def norm_forward(values, gain_vec, shift_vec):
    row_mean = jnp.mean(values, axis=-1, keepdims=True)
    centred = values - row_mean
    inv_scale = lax.rsqrt(jnp.mean(centred * centred, axis=-1, keepdims=True) + EPS)
    unit_rows = centred * inv_scale
    return (unit_rows * gain_vec + shift_vec, unit_rows, inv_scale)


def norm_backward(grad_out, unit_rows, inv_scale, gain_vec):
    scaled = grad_out * gain_vec
    grad_in = inv_scale * (
        scaled
        - jnp.mean(scaled, axis=-1, keepdims=True)
        - unit_rows * jnp.mean(scaled * unit_rows, axis=-1, keepdims=True)
    )
    return (
        grad_in,
        jnp.sum(grad_out * unit_rows, axis=0, keepdims=True),
        jnp.sum(grad_out, axis=0, keepdims=True),
    )


def swish_slope(values):
    logistic = jax.nn.sigmoid(values)
    return logistic * (1.0 + values * (1.0 - logistic))


def split_halves(local):
    odd = lax.axis_index("mp") % 2
    first = lax.dynamic_index_in_dim(local, odd, 0, keepdims=False)
    second = lax.dynamic_index_in_dim(local, 1 - odd, 0, keepdims=False)
    return first, second


def send_halves(first, second):
    count = lax.axis_size("mp")
    group = count // 2
    straight = [(i, i // 2 + (group if i % 2 else 0)) for i in range(count)]
    crossed = [(i, i // 2 + (0 if i % 2 else group)) for i in range(count)]
    return lax.ppermute(first, "mp", straight), lax.ppermute(second, "mp", crossed)


def join_halves(got_a, got_b):
    low_half = lax.axis_index("mp") < lax.axis_size("mp") // 2
    lower = jnp.where(low_half, got_a, got_b)
    upper = jnp.where(low_half, got_b, got_a)
    return jnp.concatenate([lower, upper], axis=0)


def send_back(rows):
    count = lax.axis_size("mp")
    group = count // 2
    half = lax.axis_index("mp") // group
    frames = rows.shape[0] // 2
    lower, upper = rows[:frames], rows[frames:]
    straight = [(i // 2 + (group if i % 2 else 0), i) for i in range(count)]
    crossed = [(i // 2 + (0 if i % 2 else group), i) for i in range(count)]
    return (
        lax.ppermute(jnp.where(half == 0, lower, upper), "mp", straight),
        lax.ppermute(jnp.where(half == 0, upper, lower), "mp", crossed),
    )


def join_back(got_a, got_b):
    even = lax.axis_index("mp") % 2 == 0
    return jnp.stack([jnp.where(even, got_a, got_b), jnp.where(even, got_b, got_a)]).astype(F32)


hold = lax.optimization_barrier


def rounds_fit():
    return lax.axis_size("dp") == 4 and lax.axis_size("mp") == 8


def add_rounded(one, two):
    return (one.astype(F32) + two.astype(F32)).astype(BF)


def reordered(parts, index):
    count = parts.shape[0]
    return jnp.concatenate(
        [lax.dynamic_slice_in_dim(parts, k ^ index, 1, axis=0) for k in range(count)], axis=0
    )


def joined_z(parts):
    stacked = jnp.stack([parts[r] for r in sorted(parts)])
    ordered = jnp.moveaxis(reordered(stacked, lax.axis_index("mp") // 2), 0, 1)
    return ordered.reshape(-1, *ordered.shape[2:])


def spread_z(piece):
    parts = {0: piece}
    for bit in reversed(bits_of(lax.axis_size("mp"))[1:]):
        for index in list(parts):
            parts[index | bit] = swap(parts[index], "mp", bit)
    return parts


def spread_dp(pair):
    count = lax.axis_size("dp")
    if count != 4:
        for bit in bits_of(count):
            pair = jnp.concatenate([pair, swap(pair, "dp", bit)], axis=1)
        return pair
    by_x, by_y = hold((swap(pair, "dp", 1), swap(pair, "dp", 2)))
    both = jnp.stack([swap(by_y[0], "dp", 1), swap(by_x[1], "dp", 2)])
    return jnp.concatenate([pair, by_x, by_y, both], axis=1)


def spread_small(small):
    for bit in bits_of(lax.axis_size("mp")):
        small = jnp.concatenate([small, swap(small, "mp", bit)], axis=0)
    return small


def spread_rounds(piece, middle, late, halves, far_weight, extras):
    far_bit = lax.axis_size("mp") // 2
    if not rounds_fit():
        parts = spread_z(piece)
        near, far = (
            spread_dp(
                jnp.concatenate([parts[r] for r in sorted(parts) if (r & far_bit) == want], axis=1)
            )
            for want in (0, far_bit)
        )
        blocks = (near, swap(near, "mp", 1), far, swap(far, "mp", 1))
        return (
            blocks,
            joined_z(spread_z(middle)),
            joined_z(spread_z(late)),
            send_halves(*halves),
            swap(far_weight, "mp", far_bit),
            (spread_small(extras[0]), *extras[1:]),
        )
    small, rest = extras[0], list(extras[1:])
    near, far, middle, got, *rest = hold(
        (
            swap(piece, "mp", 2),
            swap(piece, "mp", 4),
            middle,
            swap(small, "mp", 1),
            *rest,
        )
    )
    small = jnp.concatenate([small, got], axis=0)
    part_a = jnp.concatenate([piece, near], axis=1)
    a_x, a_y, far_near, mid_near, mid_far, late, far_weight, got = hold(
        (
            swap(part_a, "dp", 1),
            swap(part_a, "dp", 2),
            swap(far, "mp", 2),
            swap(middle, "mp", 2),
            swap(middle, "mp", 4),
            late,
            far_weight,
            swap(small, "mp", 2),
        )
    )
    small = jnp.concatenate([small, got], axis=0)
    part_b = jnp.concatenate([far, far_near], axis=1)
    b_x, b_y, a_0, a_1, mid_both, late_near, late, far_weight, got, *halves = hold(
        (
            swap(part_b, "dp", 1),
            swap(part_b, "dp", 2),
            swap(a_y[0], "dp", 1),
            swap(a_x[1], "dp", 2),
            swap(mid_far, "mp", 2),
            swap(late, "mp", 2),
            late,
            swap(far_weight, "mp", 4),
            swap(small, "mp", 4),
            *halves,
        )
    )
    small = jnp.concatenate([small, got], axis=0)
    all_a = jnp.concatenate([part_a, a_x, a_y, jnp.stack([a_0, a_1])], axis=1)
    b_0, b_1, other_a, late, *halves = hold(
        (
            swap(b_y[0], "dp", 1),
            swap(b_x[1], "dp", 2),
            swap(all_a, "mp", 1),
            late,
            *send_halves(*halves),
        )
    )
    all_b = jnp.concatenate([part_b, b_x, b_y, jnp.stack([b_0, b_1])], axis=1)
    return (
        (all_a, other_a, all_b, swap(all_b, "mp", 1)),
        joined_z({0: middle, 2: mid_near, 4: mid_far, 6: mid_both}),
        (late, late_near),
        halves,
        far_weight,
        (small, *rest),
    )


def z_groups():
    count = lax.axis_size("mp")
    return [list(range(core, count, 2)) for core in range(2)]


def collect_z_relative(parts):
    live = {2 * k: parts[k] for k in range(parts.shape[0])}
    for bit in bits_of(lax.axis_size("mp"))[1:]:
        for index in [r for r in live if r & bit]:
            live[index ^ bit] = add_rounded(live[index ^ bit], swap(live.pop(index), "mp", bit))
    return live[0]


def halve_z(parts, bit):
    return add_rounded(parts[0::2], swap(parts[1::2], "mp", bit))


def collect_dp(pair):
    for bit in reversed(bits_of(lax.axis_size("dp"))):
        rows = pair.shape[1] // 2
        pair = add_rounded(pair[:, :rows], swap(pair[:, rows:], "dp", bit))
    return pair


def corners(parts):
    half = parts[3].shape[0] // 2
    return swap(parts[3][:half], "dp", 1), swap(parts[3][half:], "dp", 2)


def sides(parts, to_x, to_y):
    half = parts[0].shape[0] // 2
    via_x = jnp.concatenate([parts[1][:half], add_rounded(parts[1][half:], to_y)], axis=0)
    via_y = jnp.concatenate([add_rounded(parts[2][:half], to_x), parts[2][half:]], axis=0)
    return swap(via_x, "dp", 1), swap(via_y, "dp", 2)


def finish(parts, got_x, got_y):
    return (parts[0].astype(F32) + got_x.astype(F32) + got_y.astype(F32)).astype(BF)


def collect_plain(grads_in, grads_out, z_parts, far_part):
    far_bit = lax.axis_size("mp") // 2
    sums = []
    for far in (0, 1):
        own, other = (jnp.stack([grads_in[2 * far + k], grads_out[2 * far + k]]) for k in range(2))
        sums.append(collect_dp(add_rounded(own, swap(other, "mp", 1))))
    count = lax.axis_size("mp") // 4
    stacked = jnp.concatenate([jnp.stack(jnp.split(part, count, axis=1)) for part in sums], axis=0)
    own = collect_z_relative(stacked)
    own = jnp.concatenate(
        [
            own.reshape(-1, own.shape[-1]),
            collect_z_relative(z_parts),
            add_rounded(far_part[0], swap(far_part[1], "mp", far_bit)),
        ],
        axis=0,
    )
    for bit in bits_of(lax.axis_size("dp")):
        own = jnp.concatenate([own, swap(own, "dp", bit)], axis=0)
    return own.reshape(lax.axis_size("dp"), -1, own.shape[-1])


def combine_everywhere(rows, combine, beside=None):
    step = 0
    for axis in ("dp", "mp"):
        for bit in bits_of(lax.axis_size(axis)):
            got = swap(rows, axis, bit)
            if beside is not None and step < len(beside):
                got, beside[step] = hold((got, beside[step]))
                step += 1
            rows = combine(rows, got)
    return rows


def ffn_forward(resid, gain_vec, shift_vec, blocks, b_out, beside=None):
    normed, unit_rows, inv_scale = norm_forward(resid, gain_vec, shift_vec)
    act = normed.astype(BF)
    branch = b_out
    uppers, hiddens = [], []
    for w_in_t, w_out, b_in in blocks:
        upper = dot_nt(act, w_in_t) + b_in
        hidden = jax.nn.silu(upper).astype(BF)
        branch = branch + dot_nn(hidden, w_out)
        uppers.append(upper)
        hiddens.append(hidden)
        if beside is not None and 2 * len(uppers) == len(blocks):
            branch, beside[0] = hold((branch, beside[0]))
    return branch, (unit_rows, inv_scale, act, uppers, hiddens)


def block_backward(grad_branch, act, block, upper, hidden):
    w_in_t, w_out, _ = block
    grad_hidden = dot_nt(grad_branch, w_out)
    grad_upper = (grad_hidden * swish_slope(upper)).astype(BF)
    return (
        dot_nn(grad_upper, w_in_t),
        dot_tn(grad_upper, act).astype(BF),
        dot_tn(hidden, grad_branch).astype(BF),
        jnp.sum(grad_upper, axis=0, dtype=F32, keepdims=True),
    )


def ffn_backward(grad_resid, saved, gain_vec, blocks, between=None):
    unit_rows, inv_scale, act, uppers, hiddens = saved
    grad_branch = (0.5 * grad_resid).astype(BF)
    grad_b_out = jnp.sum(grad_branch, axis=0, dtype=F32, keepdims=True)
    grad_act = 0.0
    count = len(blocks)
    grads_in, grads_out, grads_b = [None] * count, [None] * count, [None] * count
    for k in reversed(range(count)):
        part, grads_in[k], grads_out[k], grads_b[k] = block_backward(
            grad_branch, act, blocks[k], uppers[k], hiddens[k]
        )
        grad_act = grad_act + part
        if between is not None:
            grad_act, grad_branch, grads_in[k], grads_out[k] = between(
                k, (grad_act, grad_branch, grads_in[k], grads_out[k])
            )
    grad_in, grad_gain, grad_shift = norm_backward(grad_act, unit_rows, inv_scale, gain_vec)
    return (
        grad_resid + grad_in,
        (grads_in, grads_b, grads_out),
        (grad_gain, grad_shift, grad_b_out),
    )


def pair_mask(shape, head):
    lane = lax.broadcasted_iota(jnp.int32, shape, len(shape) - 1)
    return (lane // HEAD) == head


def attend_kernel(q_ref, k_ref, v_ref, bias_ref, out_ref, lse_ref):
    query, key, value = q_ref[...], k_ref[...], v_ref[...]
    bias = bias_ref[...]
    factor = LOG2E / math.sqrt(HEAD)
    mixed, logs = [], []
    for head in range(2):
        masked = jnp.where(pair_mask(query.shape, head), query, jnp.zeros_like(query))
        scores = dot_nt(masked, key) * factor + bias
        row_max = jnp.max(scores, axis=-1, keepdims=True)
        shifted = jnp.exp2(scores - row_max)
        total = jnp.sum(shifted, axis=-1, keepdims=True)
        probs = (shifted * (1.0 / total)).astype(BF)
        mixed.append(dot_nn(probs, value))
        logs.append(row_max + jnp.log2(total))
    first = pair_mask(mixed[0].shape, 0)
    out_ref[...] = jnp.where(first, mixed[0], mixed[1]).astype(BF)
    lse_ref[...] = jnp.where(first, logs[0], logs[1])


def attend_forward(query, key, value, bias, block):
    frames, columns = query.shape
    pairs = columns // (2 * HEAD)
    rows_spec = pl.BlockSpec((block, 2 * HEAD), lambda p, i: (i, p))
    whole_spec = pl.BlockSpec((frames, 2 * HEAD), lambda p, i: (0, p))
    return pl.pallas_call(
        attend_kernel,
        grid=(pairs, frames // block),
        in_specs=[rows_spec, whole_spec, whole_spec, pl.BlockSpec((1, frames), lambda p, i: (0, 0))],
        out_specs=[rows_spec, rows_spec],
        out_shape=[
            jax.ShapeDtypeStruct((frames, columns), BF),
            jax.ShapeDtypeStruct((frames, columns), F32),
        ],
        compiler_params=pltpu.CompilerParams(vmem_limit_bytes=48 * 1024 * 1024),
        cost_estimate=pl.CostEstimate(
            flops=8 * frames * frames * columns,
            bytes_accessed=12 * frames * columns,
            transcendentals=frames * frames * columns // HEAD,
        ),
        name="attend_forward",
    )(query, key, value, bias)


def attend_back_kernel(
    q_ref, k_ref, v_ref, g_ref, lse_ref, bias_ref, dq_ref, dk_ref, dv_ref, dk_acc, dv_acc
):
    step = pl.program_id(1)
    query, key, value, grad = q_ref[...], k_ref[...], v_ref[...], g_ref[...]
    bias = bias_ref[...]
    lse = lse_ref[...]
    factor = LOG2E / math.sqrt(HEAD)
    scale = 1.0 / math.sqrt(HEAD)
    dq, dk, dv = [], [], []
    for head in range(2):
        mask = pair_mask(query.shape, head)
        query_h = jnp.where(mask, query, jnp.zeros_like(query))
        grad_h = jnp.where(mask, grad, jnp.zeros_like(grad))
        scores = dot_nt(query_h, key) * factor + bias
        probs = jnp.exp2(scores - lse[:, head * HEAD : head * HEAD + 1])
        grad_probs = dot_nt(grad_h, value)
        row_dot = jnp.sum(probs * grad_probs, axis=-1, keepdims=True)
        grad_scores = (probs * (grad_probs - row_dot)).astype(BF)
        dv.append(dot_tn(probs.astype(BF), grad_h))
        dq.append(dot_nn(grad_scores, key))
        dk.append(dot_tn(grad_scores, query_h))
    first = pair_mask(dq[0].shape, 0)
    dq_ref[...] = (jnp.where(first, dq[0], dq[1]) * scale).astype(BF)
    new_dk = dk[0] + dk[1]
    new_dv = dv[0] + dv[1]

    @pl.when(step == 0)
    def _():
        dk_acc[...] = new_dk
        dv_acc[...] = new_dv

    @pl.when(step > 0)
    def _():
        dk_acc[...] += new_dk
        dv_acc[...] += new_dv

    @pl.when(step == pl.num_programs(1) - 1)
    def _():
        dk_ref[...] = (dk_acc[...] * scale).astype(BF)
        dv_ref[...] = dv_acc[...].astype(BF)


def attend_backward(query, key, value, grad, lse, bias, block):
    frames, columns = query.shape
    pairs = columns // (2 * HEAD)
    rows_spec = pl.BlockSpec((block, 2 * HEAD), lambda p, i: (i, p))
    whole_spec = pl.BlockSpec((frames, 2 * HEAD), lambda p, i: (0, p))
    shape = jax.ShapeDtypeStruct((frames, columns), BF)
    return pl.pallas_call(
        attend_back_kernel,
        grid=(pairs, frames // block),
        in_specs=[
            rows_spec,
            whole_spec,
            whole_spec,
            rows_spec,
            rows_spec,
            pl.BlockSpec((1, frames), lambda p, i: (0, 0)),
        ],
        out_specs=[rows_spec, whole_spec, whole_spec],
        out_shape=[shape, shape, shape],
        scratch_shapes=[
            pltpu.VMEM((frames, 2 * HEAD), F32),
            pltpu.VMEM((frames, 2 * HEAD), F32),
        ],
        compiler_params=pltpu.CompilerParams(vmem_limit_bytes=48 * 1024 * 1024),
        cost_estimate=pl.CostEstimate(
            flops=20 * frames * frames * columns,
            bytes_accessed=20 * frames * columns,
            transcendentals=frames * frames * columns // HEAD,
        ),
        name="attend_backward",
    )(query, key, value, grad, lse, bias)


def add_parts_kernel(one_ref, got_one_ref, two_ref, got_two_ref, out_ref):
    out_ref[0] = (one_ref[...].astype(F32) + got_one_ref[...].astype(F32)).astype(BF)
    out_ref[1] = (two_ref[...].astype(F32) + got_two_ref[...].astype(F32)).astype(BF)


def add_parts(one, got_one, two, got_two, parts):
    rows, width = one.shape
    part = rows // parts
    step = math.gcd(part, 256)
    steps = part // step
    spec = pl.BlockSpec((step, width), lambda p, j: (p * steps + j, 0))
    return pl.pallas_call(
        add_parts_kernel,
        grid=(parts, steps),
        in_specs=[spec] * 4,
        out_specs=pl.BlockSpec((None, 2, step, width), lambda p, j: (p, 0, j, 0)),
        out_shape=jax.ShapeDtypeStruct((parts, 2, part, width), BF),
        compiler_params=pltpu.CompilerParams(vmem_limit_bytes=32 * 1024 * 1024),
        cost_estimate=pl.CostEstimate(
            flops=2 * rows * width, bytes_accessed=12 * rows * width, transcendentals=0
        ),
        name="add_parts",
    )(one, got_one, two, got_two)


def unpack_kernel(index_ref, part_ref, in_ref, out_ref):
    rows = out_ref.shape[0]
    in_ref[...] = part_ref[:rows].astype(F32).T
    out_ref[...] = part_ref[rows:].astype(F32)


def unpack(parts, index, rows, place):
    count, _, width = parts.shape
    return pl.pallas_call(
        unpack_kernel,
        grid_spec=pltpu.PrefetchScalarGridSpec(
            num_scalar_prefetch=1,
            grid=(count,),
            in_specs=[
                pl.BlockSpec((None, 2 * rows, width), lambda r, at: (r, place // (2 * rows), 0))
            ],
            out_specs=[
                pl.BlockSpec((width, rows), lambda r, at: (0, at[0] ^ r)),
                pl.BlockSpec((rows, width), lambda r, at: (at[0] ^ r, 0)),
            ],
        ),
        out_shape=[
            jax.ShapeDtypeStruct((width, count * rows), F32),
            jax.ShapeDtypeStruct((count * rows, width), F32),
        ],
        compiler_params=pltpu.CompilerParams(vmem_limit_bytes=32 * 1024 * 1024),
        cost_estimate=pl.CostEstimate(
            flops=0, bytes_accessed=12 * count * rows * width, transcendentals=0
        ),
        name="unpack",
    )(index.reshape(1), parts)


def lay_out(buffer, before, rows, after, halo):
    count = rows.shape[0]
    buffer[:halo] = before[...]
    buffer[halo : halo + count] = rows[...]
    buffer[halo + count :] = after[...]


def depth_kernel(
    before_ref, rows_ref, after_ref, taps_ref, visible_ref, depth_ref, stats_ref, padded, *, taps
):
    count, lanes = depth_ref.shape
    halo = before_ref.shape[0]
    first = halo - taps // 2
    lay_out(padded, before_ref, rows_ref, after_ref, halo)
    depth = jnp.zeros((count, lanes), F32)
    for phase in range(8):
        more = (taps - 1 - phase) // 8
        base = padded[first + phase : first + phase + count + 8 * more]
        for step in range(more + 1):
            tap = 8 * step + phase
            depth = depth + base[8 * step : 8 * step + count] * taps_ref[tap : tap + 1]
    depth_ref[...] = depth
    visible = visible_ref[...]
    frames = jnp.sum(visible, axis=0, keepdims=True)
    mean = jnp.sum(depth * visible, axis=0, keepdims=True) / jnp.maximum(frames, 1.0)
    apart = (depth - mean) * visible
    stats_ref[0:1] = jnp.broadcast_to(frames, (1, lanes))
    stats_ref[1:2] = mean
    stats_ref[2:3] = jnp.sum(apart * apart, axis=0, keepdims=True)
    stats_ref[3:] = jnp.zeros((5, lanes), F32)


def depth_forward(rows, around, taps_rows, visible, taps):
    count, width = rows.shape
    lanes = 128
    halo = around[0].shape[0]

    def column(height):
        return pl.BlockSpec((height, lanes), lambda j: (0, j))

    return pl.pallas_call(
        functools.partial(depth_kernel, taps=taps),
        grid=(width // lanes,),
        in_specs=[
            column(halo),
            column(count),
            column(halo),
            column(taps_rows.shape[0]),
            pl.BlockSpec((count, 1), lambda j: (0, 0)),
        ],
        out_specs=[column(count), column(8)],
        out_shape=[
            jax.ShapeDtypeStruct((count, width), F32),
            jax.ShapeDtypeStruct((8, width), F32),
        ],
        scratch_shapes=[pltpu.VMEM((count + 2 * halo, lanes), F32)],
        cost_estimate=pl.CostEstimate(
            flops=2 * taps * count * width, bytes_accessed=9 * count * width, transcendentals=0
        ),
        name="depth_forward",
    )(around[0], rows, around[1], taps_rows, visible)


def depth_back_kernel(
    gbefore_ref,
    grad_ref,
    gafter_ref,
    before_ref,
    rows_ref,
    after_ref,
    taps_ref,
    visible_ref,
    value_ref,
    logistic_ref,
    gvalue_ref,
    ggate_ref,
    gtaps_ref,
    gbias_ref,
    gpadded,
    padded,
    *,
    taps,
):
    count, lanes = grad_ref.shape
    halo = before_ref.shape[0]
    first = halo - taps // 2
    lay_out(gpadded, gbefore_ref, grad_ref, gafter_ref, halo)
    lay_out(padded, before_ref, rows_ref, after_ref, halo)
    grad = grad_ref[...]
    total = jnp.zeros((count, lanes), F32)
    for phase in range(8):
        more = (taps - 1 - phase) // 8
        stop = first + phase + count + 8 * more
        gbase = gpadded[first + phase : stop]
        base = padded[first + phase : stop]
        for step in range(more + 1):
            tap = 8 * step + phase
            back = taps - 1 - tap
            total = total + gbase[8 * step : 8 * step + count] * taps_ref[back : back + 1]
            product = grad * base[8 * step : 8 * step + count]
            gtaps_ref[tap : tap + 1] = jnp.sum(product, axis=0, keepdims=True)
    grad_gated = total * visible_ref[...]
    logistic = logistic_ref[...]
    gvalue = (grad_gated * logistic).astype(BF)
    ggate = (grad_gated * value_ref[...] * logistic * (1.0 - logistic)).astype(BF)
    gvalue_ref[...] = gvalue
    ggate_ref[...] = ggate
    gbias_ref[0:1] = jnp.sum(gvalue.astype(F32), axis=0, keepdims=True)
    gbias_ref[1:2] = jnp.sum(ggate.astype(F32), axis=0, keepdims=True)
    gbias_ref[2:] = jnp.zeros((6, lanes), F32)


def depth_backward(grad, garound, rows, around, taps_rows, visible, value, logistic, taps):
    count, width = rows.shape
    lanes = 128
    halo = around[0].shape[0]

    def column(height):
        return pl.BlockSpec((height, lanes), lambda j: (0, j))

    return pl.pallas_call(
        functools.partial(depth_back_kernel, taps=taps),
        grid=(width // lanes,),
        in_specs=[
            column(halo),
            column(count),
            column(halo),
            column(halo),
            column(count),
            column(halo),
            column(taps_rows.shape[0]),
            pl.BlockSpec((count, 1), lambda j: (0, 0)),
            column(count),
            column(count),
        ],
        out_specs=[column(count), column(count), column(taps_rows.shape[0]), column(8)],
        out_shape=[
            jax.ShapeDtypeStruct((count, width), BF),
            jax.ShapeDtypeStruct((count, width), BF),
            jax.ShapeDtypeStruct(taps_rows.shape, F32),
            jax.ShapeDtypeStruct((8, width), F32),
        ],
        scratch_shapes=[pltpu.VMEM((count + 2 * halo, lanes), F32)] * 2,
        cost_estimate=pl.CostEstimate(
            flops=4 * taps * count * width, bytes_accessed=24 * count * width, transcendentals=0
        ),
        name="depth_backward",
    )(
        garound[0], grad, garound[1], around[0], rows, around[1], taps_rows, visible, value, logistic
    )


def spread_blocks(local, group):
    blocks = {0: local}
    for bit in reversed(bits_of(group)):
        for index in list(blocks):
            blocks[index | bit] = swap(blocks[index], "mp", bit)
    return [blocks[r] for r in range(group)]


def collect_blocks(parts):
    live = dict(enumerate(parts))
    for bit in bits_of(len(parts)):
        for index in [r for r in live if not r & bit]:
            sent = swap(live.pop(index | bit).astype(BF), "mp", bit)
            live[index] = live[index] + sent.astype(F32)
    return live[0]


def exchange_blocks(parts):
    return [parts[0]] + [swap(parts[r], "mp", r) for r in range(1, len(parts))]


def shards(
    frames,
    lengths,
    mask_flags,
    mask_embed,
    ffa_gain,
    ffa_shift,
    ffa_w_in,
    ffa_b_in,
    ffa_w_out,
    ffa_b_out,
    att_gain,
    att_shift,
    att_w_qkv,
    att_b_qv,
    att_w_out,
    att_b_out,
    conv_gain,
    conv_shift,
    conv_w_in,
    conv_b_in,
    conv_w_depth,
    batch_scale,
    batch_shift,
    running_mean,
    running_var,
    conv_w_out,
    conv_b_out,
    ffb_gain,
    ffb_shift,
    ffb_w_in,
    ffb_b_in,
    ffb_w_out,
    ffb_b_out,
    final_gain,
    final_shift,
    cotangent,
):
    mask_embed = mask_embed[None]
    ffa_gain = ffa_gain[None]
    ffa_shift = ffa_shift[None]
    ffa_b_out = ffa_b_out[None]
    att_gain = att_gain[None]
    att_shift = att_shift[None]
    att_b_out = att_b_out[None]
    conv_gain = conv_gain[None]
    conv_shift = conv_shift[None]
    conv_b_out = conv_b_out[None]
    ffb_gain = ffb_gain[None]
    ffb_shift = ffb_shift[None]
    ffb_b_out = ffb_b_out[None]
    final_gain = final_gain[None]
    final_shift = final_shift[None]
    dp = lax.axis_size("dp")
    mp = lax.axis_size("mp")
    zs = mp // 2
    group = mp // 2
    d = lax.axis_index("dp")
    m = lax.axis_index("mp")
    core = m % 2
    half = m // group
    q = m % group
    width = frames.shape[2]
    columns = width // mp
    rows_local = 2 * frames.shape[1]
    hidden_q = ffa_b_in.shape[0] // dp
    chan_q = columns // dp
    taps = conv_w_depth.shape[0]
    reach = taps // 2

    small = jnp.concatenate(
        [
            ffa_b_in.astype(F32).reshape(-1, columns),
            ffb_b_in.astype(F32).reshape(-1, columns),
            conv_b_in,
            conv_w_depth,
            batch_scale[None],
            batch_shift[None],
        ],
        axis=0,
    )
    per = ffa_b_in.shape[0] // columns
    low = mp // 4

    def relative_bias(far, near_core):
        first = far * (mp // 2) + near_core
        part = bias_rel[first : first + 2 * low : 2]
        return part.transpose(1, 0, 2).reshape(1, -1)


    def hidden_bias(rows):
        both = rows.reshape(zs, 2, dp * hidden_q).transpose(1, 0, 2).reshape(2, -1)
        own = lax.dynamic_slice_in_dim(both, core, 1, axis=0)
        other = lax.dynamic_slice_in_dim(both, 1 - core, 1, axis=0)
        return own, other

    def to_canon(rows):
        lead = rows.shape[:-1]
        split = rows.reshape(*lead, zs, 2, columns)
        return jnp.moveaxis(split, -3, -2).reshape(*lead, width)

    def from_canon(rows):
        lead = rows.shape[:-1]
        split = rows.reshape(*lead, 2, zs, columns)
        return jnp.moveaxis(split, -3, -2).reshape(*lead, width)

    def own_columns(rows):
        return lax.dynamic_slice_in_dim(rows, m * columns, columns, axis=-1)

    def hidden_pieces(w_in, w_out):
        piece_in = lax.dynamic_slice_in_dim(w_in, d * hidden_q, hidden_q, axis=1).T
        piece_out = lax.dynamic_slice_in_dim(w_out, d * hidden_q, hidden_q, axis=0)
        return piece_in, piece_out

    def channel_piece(rows):
        return lax.dynamic_slice_in_dim(rows, d * chan_q, chan_q, axis=0)

    kinds = [conv_w_in[0].T, conv_w_in[1].T, conv_w_out, att_w_out]
    valid_count = jnp.sum(lengths).astype(F32)
    for bit in bits_of(dp):
        valid_count = valid_count + swap(valid_count, "dp", bit)
    gathered, mid_z, late_z, halves, w_other, extras = spread_rounds(
        jnp.stack(hidden_pieces(ffa_w_in, ffa_w_out)),
        jnp.stack([channel_piece(rows) for rows in kinds]),
        jnp.stack(hidden_pieces(ffb_w_in, ffb_w_out)),
        split_halves(frames),
        att_w_qkv,
        (
            small[None],
            swap(att_b_qv, "mp", group),
            join_halves(*send_halves(*split_halves(mask_flags))),
            valid_count,
        ),
    )
    small, b_other, flag_rows, valid_count = extras
    bias_rel = small[:, :per].reshape(mp, dp, hidden_q)[:, jnp.arange(dp) ^ d]
    small = small[jnp.arange(mp) ^ m]
    bias_b = hidden_bias(small[:, per : 2 * per])
    conv_small = to_canon(jnp.moveaxis(small[:, 2 * per :], 0, 1).reshape(-1, width))
    rows_in = join_halves(*halves)
    flag_rows = flag_rows.astype(F32)[:, None]
    c_b_in = [conv_small[0:1], conv_small[1:2]]
    c_depth = jnp.pad(conv_small[2 : 2 + taps], ((0, -taps % 8), (0, 0)))
    c_scale = conv_small[2 + taps : 3 + taps]
    c_shift = conv_small[3 + taps : 4 + taps]
    blocks_a = [
        (gathered[k][0], gathered[k][1], relative_bias(k // 2, k % 2)) for k in range(4)
    ]
    mid_own = lax.all_gather(mid_z, "dp", axis=1, tiled=True)

    w_qkv = jnp.concatenate(
        [jnp.where(half == 0, att_w_qkv, w_other), jnp.where(half == 0, w_other, att_w_qkv)], axis=2
    )
    b_qv = jnp.concatenate(
        [jnp.where(half == 0, att_b_qv, b_other), jnp.where(half == 0, b_other, att_b_qv)], axis=1
    )


    length = lax.dynamic_index_in_dim(lengths, half, 0, keepdims=False)
    place = q * rows_local + jnp.arange(rows_local)
    visible = (place < length).astype(F32)[:, None]
    key_place = ((jnp.arange(group) ^ q)[:, None] * rows_local + jnp.arange(rows_local)).reshape(1, -1)
    key_bias = jnp.where(key_place < length, 0.0, -1e30).astype(F32)

    resid_a = rows_in.astype(F32) + flag_rows * mask_embed
    beside = [swap(late_z[0], "mp", 4)] if rounds_fit() else None
    branch, saved_a = ffn_forward(resid_a, ffa_gain, ffa_shift, blocks_a, ffa_b_out, beside)
    resid_b = resid_a + 0.5 * branch

    normed, att_unit, att_inv = norm_forward(resid_b, att_gain, att_shift)
    blocks = spread_blocks(normed.astype(BF), group)
    *blocks, mid_own, beside = hold((*blocks, mid_own, beside))
    if rounds_fit():
        far_near = swap(beside[0], "mp", 2)
    mid_other = swap(mid_own, "mp", 1)
    att_rows = jnp.concatenate(blocks, axis=0)
    query = (dot_nn(att_rows, w_qkv[0]) + b_qv[0]).astype(BF)
    key = dot_nn(att_rows, w_qkv[1]).astype(BF)
    value = (dot_nn(att_rows, w_qkv[2]) + b_qv[1]).astype(BF)
    if rounds_fit():
        query, key, value, far_near = hold((query, key, value, far_near))
        late_z = joined_z({0: late_z[0], 2: late_z[1], 4: beside[0], 6: far_near})
    late_own = lax.all_gather(late_z, "dp", axis=1, tiled=True)
    block = rows_local
    mixed_cols, lse = attend_forward(query, key, value, key_bias, block)
    parts = [mixed_cols[r * rows_local : (r + 1) * rows_local] for r in range(group)]
    parts = exchange_blocks(parts)
    mid = jnp.stack(
        [
            jnp.where(core == 0, one, two).reshape(4, zs, columns, width)
            for one, two in ((mid_own, mid_other), (mid_other, mid_own))
        ],
        axis=1,
    )
    conv_value_w, conv_gate_w, conv_out_w = (mid[k].reshape(width, width) for k in range(3))
    att_out_w = mid[3].transpose(1, 0, 2, 3).reshape(2, group, columns, width)
    att_out_w = reordered(jnp.moveaxis(att_out_w, 1, 0), q).reshape(width, width)
    *parts, conv_value_w, conv_gate_w, conv_out_w, att_out_w, cotangent = hold(
        (*parts, conv_value_w, conv_gate_w, conv_out_w, att_out_w, cotangent)
    )
    cot_halves = send_halves(*split_halves(cotangent))
    mixed = jnp.concatenate(parts, axis=1)
    resid_c = resid_b + (dot_nn(mixed, att_out_w) + att_b_out)

    normed, conv_unit, conv_inv = norm_forward(resid_c, conv_gain, conv_shift)
    conv_act = normed.astype(BF)
    pre_value = dot_nt(conv_act, conv_value_w) + c_b_in[0]
    pre_gate = dot_nt(conv_act, conv_gate_w) + c_b_in[1]
    logistic = jax.nn.sigmoid(pre_gate)
    gated = pre_value * logistic * visible

    up = [(i, i + 1) for i in range(mp - 1) if (i + 1) % group]
    down = [(i + 1, i) for i, _ in up]

    halo = -(-reach // 8) * 8

    def halos(rows):
        return lax.ppermute(rows[-halo:], "mp", up), lax.ppermute(rows[:halo], "mp", down)

    gated_halos = halos(gated)
    depth, stats = depth_forward(gated, gated_halos, c_depth, visible, taps)
    depth, stats, late_own, *cot_halves = hold((depth, stats, late_own, *cot_halves))
    cot_rows = join_halves(*cot_halves)
    late_own = late_own.reshape(2, -1, width)
    late_other = swap(late_own, "mp", 1)
    blocks_b = [(late_own[0], late_own[1], bias_b[0]), (late_other[0], late_other[1], bias_b[1])]

    def join(one, two):
        both = jnp.maximum(one[0:1] + two[0:1], 1.0)
        gap = one[1:2] - two[1:2]
        return jnp.concatenate(
            [
                one[0:1] + two[0:1],
                (one[0:1] * one[1:2] + two[0:1] * two[1:2]) / both,
                one[2:3] + two[2:3] + gap * gap * (one[0:1] * two[0:1] / both),
                one[3:],
            ],
            axis=0,
        )

    stats = combine_everywhere(stats, join)
    batch_mean = stats[1:2]
    batch_var = stats[2:3] / valid_count
    inv_batch = lax.rsqrt(batch_var + EPS)
    centred = depth - batch_mean
    normed_bn = centred * inv_batch * c_scale + c_shift
    swished = jax.nn.silu(normed_bn).astype(BF)
    resid_d = resid_c + (dot_nn(swished, conv_out_w) + conv_b_out)

    branch, saved_b = ffn_forward(resid_d, ffb_gain, ffb_shift, blocks_b, ffb_b_out)
    resid_e = resid_d + 0.5 * branch
    layer_rows, unit_out, inv_out = norm_forward(resid_e, final_gain, final_shift)

    grad_resid, g_final_gain, g_final_shift = norm_backward(
        cot_rows.astype(F32), unit_out, inv_out, final_gain
    )
    grad_resid, mats_b, vecs_b = ffn_backward(grad_resid, saved_b, ffb_gain, blocks_b)

    def by_core(rows):
        part = width // 2
        return [
            lax.dynamic_slice_in_dim(rows, which * part, part, axis=1) for which in (core, 1 - core)
        ]

    grad_branch = grad_resid.astype(BF)
    g_conv_b_out = jnp.sum(grad_branch, axis=0, dtype=F32, keepdims=True)
    grad_normed = dot_nt(grad_branch, conv_out_w) * swish_slope(normed_bn)
    g_conv_out = [dot_tn(rows, grad_branch).astype(BF) for rows in by_core(swished)]
    sums = jnp.concatenate(
        [
            jnp.sum(grad_normed, axis=0, keepdims=True),
            jnp.sum(grad_normed * centred, axis=0, keepdims=True),
        ],
        axis=0,
    )
    late_g = [mats_b[0][1], mats_b[2][1], mats_b[0][0], mats_b[2][0]]
    sums = combine_everywhere(sums, jnp.add, late_g)
    late_got = [swap(grads, "mp", 1) for grads in late_g[:2]]
    sums, layer_rows = hold((sums, layer_rows.astype(BF)))
    layer_out = send_back(layer_rows)
    grad_normed, *late_got = hold((grad_normed, *late_got))
    late_sum = add_parts(late_g[2], late_got[0], late_g[3], late_got[1], 1)
    late_sum = late_sum.reshape(2 * zs, dp * hidden_q, width)
    late_sum = lax.psum_scatter(late_sum, "dp", scatter_dimension=1, tiled=True)
    inv_cube = inv_batch * inv_batch * inv_batch
    grad_depth = grad_normed * (c_scale * inv_batch) - visible * (
        (inv_batch * c_scale * sums[0:1] + inv_cube * c_scale * sums[1:2] * centred) / valid_count
    )
    grad_value_pre, grad_gate_pre, g_depth, g_conv_b_in = depth_backward(
        grad_depth,
        halos(grad_depth),
        gated,
        gated_halos,
        c_depth,
        visible,
        pre_value,
        logistic,
        taps,
    )
    grad_act = dot_nn(grad_value_pre, conv_value_w) + dot_nn(grad_gate_pre, conv_gate_w)
    g_conv_value = [dot_tn(rows, conv_act).astype(BF) for rows in by_core(grad_value_pre)]
    g_conv_gate = [dot_tn(rows, conv_act).astype(BF) for rows in by_core(grad_gate_pre)]
    grad_in, g_conv_gain, g_conv_shift = norm_backward(grad_act, conv_unit, conv_inv, conv_gain)
    grad_resid = grad_resid + grad_in

    grad_branch = grad_resid.astype(BF)
    g_att_b_out = jnp.sum(grad_branch, axis=0, dtype=F32, keepdims=True)
    grad_mixed = dot_nt(grad_branch, att_out_w).astype(BF)
    g_att_out = []
    for which in range(2):
        one = [
            lax.dynamic_slice_in_dim(
                mixed,
                ((((q // 2) ^ k) * 2 + which) * 2 + slot) * columns,
                columns,
                axis=1,
            )
            for slot in range(2)
            for k in range(group // 2)
        ]
        g_att_out.append(dot_tn(jnp.concatenate(one, axis=1), grad_branch).astype(BF))
    wide = 2 * columns
    parts = [grad_mixed[:, r * wide : (r + 1) * wide] for r in range(group)]
    grad_cols = jnp.concatenate(exchange_blocks(parts), axis=0)
    grad_q, grad_k, grad_v = attend_backward(query, key, value, grad_cols, lse, key_bias, block // 2)

    mid_g = [g_conv_value, g_conv_gate, g_conv_out, g_att_out]
    mid_got = swap(jnp.concatenate([g[1] for g in mid_g], axis=0), "mp", 1)
    grad_all = jnp.concatenate([grad_q, grad_k, grad_v], axis=1)
    w_flat = jnp.concatenate([w_qkv[0], w_qkv[1], w_qkv[2]], axis=1)
    partial = dot_nt(grad_all, w_flat)
    g_qkv = dot_tn(grad_all, att_rows).astype(BF)
    partial, g_qkv, mid_got, *layer_out = hold((partial, g_qkv, mid_got, *layer_out))
    mid_got = mid_got.reshape(4, zs, columns, width)
    joint = [
        add_rounded(g[0].reshape(zs, columns, width), got)
        for g, got in zip(mid_g, mid_got, strict=True)
    ] + [g_qkv.reshape(6, columns, width)]
    joint_rows = (4 * zs + 6) * chan_q
    if rounds_fit():
        joint_parts = []
        for r in range(dp):
            part = [
                lax.dynamic_slice_in_dim(rows, (d ^ r) * chan_q, chan_q, axis=1) for rows in joint
            ]
            joint_parts.append(jnp.concatenate(part, axis=0).reshape(joint_rows, width))
        joint_corners = corners(joint_parts)
    grad_act = collect_blocks(
        [partial[r * rows_local : (r + 1) * rows_local] for r in range(group)]
    )
    if rounds_fit():
        grad_act, late_sum, *joint_corners = hold((grad_act, late_sum, *joint_corners))
        joint_sides = sides(joint_parts, *joint_corners)
    late_sum = late_sum.reshape(2, zs, hidden_q, width)
    late_parts = reordered(jnp.moveaxis(late_sum, 1, 0).reshape(zs, -1, width), m // 2)
    g_qv = jnp.stack(
        [jnp.sum(grad_q, axis=0, dtype=F32), jnp.sum(grad_v, axis=0, dtype=F32)]
    ).reshape(2, 2, 1, columns)
    g_b_qv = lax.dynamic_update_slice(
        jnp.zeros((2, 2, group, columns), F32), g_qv, (0, 0, q, 0)
    ).reshape(2, width)
    grad_in, g_att_gain, g_att_shift = norm_backward(grad_act, att_unit, att_inv, att_gain)
    grad_resid = grad_resid + grad_in

    def joint_pieces(rows):
        rows = rows.reshape(-1, chan_q, width)
        parts = jnp.moveaxis(rows[: 4 * zs].reshape(4, zs, chan_q, width), 1, 0)
        parts = reordered(parts.reshape(zs, -1, width), m // 2)
        pair = rows[4 * zs :].reshape(3, 2, chan_q, width)
        pair = [
            lax.dynamic_index_in_dim(pair, which, 1, keepdims=False).reshape(-1, width)
            for which in (half, 1 - half)
        ]
        return parts, pair

    flight = {}

    def between(k, held):
        if k == 3:
            held = hold(held)
            flight["b"] = [swap(held[2], "mp", 1), swap(held[3], "mp", 1)]
            flight["late"] = swap(late_parts[1::2], "mp", 2)
        elif k == 2:
            *held, b_in, b_out, side_x, side_y, late_got = hold(
                (*held, *flight["b"], *joint_sides, flight["late"])
            )
            parts = add_parts(held[2], b_in, held[3], b_out, 4)
            flight["b_parts"] = [parts[r].reshape(-1, width) for r in range(4)]
            flight["corners"] = corners(flight["b_parts"])
            late = add_rounded(late_parts[0::2], late_got)
            flight["late"] = [late[0], swap(late[1], "mp", 4)]
            flight["mid"], flight["pair"] = joint_pieces(finish(joint_parts, side_x, side_y))
        elif k == 1:
            mid = flight["mid"]
            *held, to_x, to_y, far = hold((*held, *flight["corners"], flight["late"][1]))
            flight["sides"] = sides(flight["b_parts"], to_x, to_y)
            flight["late"] = add_rounded(flight["late"][0], far)
            flight["a"] = [swap(held[2], "mp", 1), swap(held[3], "mp", 1)]
            flight["mid_got"] = swap(mid[1::2], "mp", 2)
        else:
            *held, a_in, a_out, mid_got = hold((*held, *flight["a"], flight["mid_got"]))
            parts = add_parts(held[2], a_in, held[3], a_out, 4)
            flight["a_parts"] = [parts[r].reshape(-1, width) for r in range(4)]
            flight["corners"] = corners(flight["a_parts"])
            mid = add_rounded(flight["mid"][0::2], mid_got)
            rows = jnp.concatenate([mid[1], flight["pair"][1]], axis=0)
            flight["far"] = [
                jnp.concatenate([mid[0], flight["pair"][0]], axis=0),
                swap(rows, "mp", 4),
            ]
        return held

    grad_resid, mats_a, vecs_a = ffn_backward(
        grad_resid, saved_a, ffa_gain, blocks_a, between if rounds_fit() else None
    )
    g_embed = jnp.sum(grad_resid * flag_rows, axis=0, keepdims=True)
    grad_frames = send_back(grad_resid.astype(BF))

    def hidden_order(parts):
        own, other = parts
        both = jnp.stack([jnp.where(core == 0, own, other), jnp.where(core == 0, other, own)])
        return both.reshape(2, zs, dp * hidden_q).transpose(1, 0, 2).reshape(-1, width)

    def relative_order(parts):
        rel = jnp.stack(parts).reshape(2, 2, dp, low, hidden_q)
        rel = rel.transpose(0, 3, 1, 2, 4).reshape(mp, dp, hidden_q)
        return rel[jnp.arange(mp) ^ m][:, jnp.arange(dp) ^ d].reshape(-1, width)

    small = (
        jnp.concatenate(
            [
                from_canon(jnp.concatenate([g_depth[:taps], g_conv_b_in[:2]], axis=0)),
                hidden_order(mats_b[1]),
                relative_order(mats_a[1]),
                g_b_qv,
                *vecs_b,
                g_final_gain,
                g_final_shift,
                g_conv_b_out,
                g_conv_gain,
                g_conv_shift,
                *vecs_a,
                g_embed,
                g_att_b_out,
                g_att_gain,
                g_att_shift,
            ],
            axis=0,
        )
    )
    if rounds_fit():
        b_x, b_y, *grad_frames, far, got = hold(
            (*flight["sides"], *grad_frames, flight["far"][1], swap(small, "dp", 1))
        )
        small = small + got
        b_sum = finish(flight["b_parts"], b_x, b_y).reshape(2, 2, hidden_q, width)
        rest = jnp.concatenate([flight["late"], add_rounded(flight["far"][0], far)], axis=0)
        to_x, to_y, b_near, got, rest = hold(
            (
                *flight["corners"],
                swap(b_sum[:, 1], "mp", 2),
                swap(small, "dp", 2),
                rest,
            )
        )
        small = small + got
        side_x, side_y = sides(flight["a_parts"], to_x, to_y)
        b_far, side_x, side_y, got, rest_x, rest_y = hold(
            (
                swap(add_rounded(b_sum[:, 0], b_near), "mp", 4),
                side_x,
                side_y,
                swap(small, "mp", 1),
                rest,
                rest,
            )
        )
        small = small + got
        a_sum = finish(flight["a_parts"], side_x, side_y).reshape(2, 2, hidden_q, width)
        a_near, got, rest_x, rest_y = hold(
            (
                swap(a_sum[:, 1], "mp", 2),
                swap(small, "mp", 2),
                swap(rest_x, "dp", 1),
                swap(rest_y, "dp", 2),
            )
        )
        small = small + got
        own = a_sum[:, 0].astype(F32) + a_near.astype(F32) + b_far.astype(F32)
        own = own.astype(BF).reshape(-1, width)
        cut = rest.shape[0] // 2
        by_x, by_y, got, rest_0, rest_1 = hold(
            (
                swap(own, "dp", 1),
                swap(own, "dp", 2),
                swap(small, "mp", 4),
                swap(rest_y[:cut], "dp", 1),
                swap(rest_x[cut:], "dp", 2),
            )
        )
        small = small + got
        corner = [swap(by_y[:hidden_q], "dp", 1), swap(by_x[hidden_q:], "dp", 2)]
        first = jnp.stack([own, by_x, by_y, jnp.concatenate(corner, axis=0)])
        rest = jnp.stack([rest, rest_x, rest_y, jnp.concatenate([rest_0, rest_1], axis=0)])
    else:
        joint = jnp.concatenate(joint, axis=0)
        joint = lax.psum_scatter(joint, "dp", scatter_dimension=1, tiled=True)
        mid_parts, pair = joint_pieces(joint)
        total = collect_plain(
            mats_a[0], mats_a[2], jnp.concatenate([late_parts, mid_parts], axis=1), pair
        )
        first, rest = total[:, : 2 * hidden_q], total[:, 2 * hidden_q :]
        small = combine_everywhere(small, jnp.add)
    if hidden_q % 128 == 0:
        g_ffa_in, g_ffa_out = unpack(first, d, hidden_q, 0)
        g_ffb_in, g_ffb_out = unpack(rest[:, : 2 * hidden_q], d, hidden_q, 0)
    else:
        pairs = []
        for part in (first, rest[:, : 2 * hidden_q]):
            part = reordered(part, d).reshape(dp, 2, hidden_q, width).astype(F32)
            part = jnp.moveaxis(part, 1, 0).reshape(2, -1, width)
            pairs += [part[0].T, part[1]]
        g_ffa_in, g_ffa_out, g_ffb_in, g_ffb_out = pairs
    rest = reordered(rest[:, 2 * hidden_q :], d).reshape(dp, 7, chan_q, width)
    rest = jnp.moveaxis(rest, 1, 0).reshape(7, columns, width).astype(F32)
    mid_total = rest[:4]
    g_att_qkv = rest[4:].transpose(0, 2, 1)

    total = small
    g_w_depth = own_columns(total[:taps])
    g_b_conv = own_columns(total[taps : taps + 2])
    at = taps + 2
    hidden_rows = mp * hidden_q * dp // width
    share = mats_b[1][0].shape[1] * 2 // mp

    def own_hidden(rows):
        return lax.dynamic_slice_in_dim(rows.reshape(-1), m * share, share, axis=0)

    g_ffb_b_in = own_hidden(total[at : at + hidden_rows])
    g_ffa_b_in = own_hidden(total[at + hidden_rows : at + 2 * hidden_rows])
    at = at + 2 * hidden_rows
    g_qv_out = own_columns(total[at : at + 2])
    e = total[at + 2 :]
    f = e[8:]

    def own_canon(vector):
        return own_columns(from_canon(vector))[0]

    mean_own = own_canon(batch_mean)
    var_own = own_canon(batch_var)
    g_scale = own_canon(sums[1:2] * inv_batch)
    g_shift = own_canon(sums[0:1])
    new_mean = 0.9 * running_mean + 0.1 * mean_own
    new_var = 0.9 * running_var + 0.1 * var_own * valid_count / (valid_count - 1.0)
    g_conv_w_in = jnp.stack([mid_total[0].T, mid_total[1].T])
    return (
        join_back(*layer_out),
        join_back(*grad_frames),
        f[3],
        f[0],
        f[1],
        g_ffa_in,
        g_ffa_b_in,
        g_ffa_out,
        f[2],
        f[5],
        f[6],
        g_att_qkv,
        g_qv_out,
        mid_total[3],
        f[4],
        e[6],
        e[7],
        g_conv_w_in,
        g_b_conv,
        g_w_depth,
        g_scale,
        g_shift,
        mid_total[2],
        e[5],
        e[0],
        e[1],
        g_ffb_in,
        g_ffb_b_in,
        g_ffb_out,
        e[2],
        e[3],
        e[4],
        new_mean,
        new_var,
    )


def solution(mesh):
    return jax.shard_map(
        shards,
        mesh=mesh,
        in_specs=(
            P("dp", "mp", None),
            P("dp"),
            P("dp", "mp"),
            P(),
            P(),
            P(),
            P(None, "mp"),
            P("mp"),
            P("mp", None),
            P(),
            P(),
            P(),
            P(None, None, "mp"),
            P(None, "mp"),
            P("mp", None),
            P(),
            P(),
            P(),
            P(None, None, "mp"),
            P(None, "mp"),
            P(None, "mp"),
            P("mp"),
            P("mp"),
            P("mp"),
            P("mp"),
            P("mp", None),
            P(),
            P(),
            P(),
            P(None, "mp"),
            P("mp"),
            P("mp", None),
            P(),
            P(),
            P(),
            P("dp", "mp", None),
        ),
        out_specs=(
            P("dp", "mp", None),
            P("dp", "mp", None),
            P(),
            P(),
            P(),
            P(None, "mp"),
            P("mp"),
            P("mp", None),
            P(),
            P(),
            P(),
            P(None, None, "mp"),
            P(None, "mp"),
            P("mp", None),
            P(),
            P(),
            P(),
            P(None, None, "mp"),
            P(None, "mp"),
            P(None, "mp"),
            P("mp"),
            P("mp"),
            P("mp", None),
            P(),
            P(),
            P(),
            P(None, "mp"),
            P("mp"),
            P("mp", None),
            P(),
            P(),
            P(),
            P("mp"),
            P("mp"),
        ),
        check_vma=False,
    )
```

```python
import functools
import math

import jax
import jax.numpy as jnp
from jax import lax
from jax.experimental import pallas as pl
from jax.experimental.pallas import tpu as pltpu
from jax.sharding import PartitionSpec as P

HEAD = 64
EPS = 1e-05
BF = jnp.bfloat16
F32 = jnp.float32
LOG2E = math.log2(math.e)


def dot_nn(left, right):
    return lax.dot_general(left, right, (((1,), (0,)), ((), ())), preferred_element_type=F32)


def dot_nt(left, right):
    return lax.dot_general(left, right, (((1,), (1,)), ((), ())), preferred_element_type=F32)


def dot_tn(left, right):
    return lax.dot_general(left, right, (((0,), (0,)), ((), ())), preferred_element_type=F32)


def swap(values, axis, bit):
    count = lax.axis_size(axis)
    return lax.ppermute(values, axis, [(i, i ^ bit) for i in range(count)])


def bits_of(count):
    return [1 << k for k in range(count.bit_length() - 1)]


def norm_forward(values, gain_vec, shift_vec):
    row_mean = jnp.mean(values, axis=-1, keepdims=True)
    centred = values - row_mean
    inv_scale = lax.rsqrt(jnp.mean(centred * centred, axis=-1, keepdims=True) + EPS)
    unit_rows = centred * inv_scale
    return (unit_rows * gain_vec + shift_vec, unit_rows, inv_scale)


def norm_backward(grad_out, unit_rows, inv_scale, gain_vec):
    scaled = grad_out * gain_vec
    grad_in = inv_scale * (
        scaled
        - jnp.mean(scaled, axis=-1, keepdims=True)
        - unit_rows * jnp.mean(scaled * unit_rows, axis=-1, keepdims=True)
    )
    return (
        grad_in,
        jnp.sum(grad_out * unit_rows, axis=0, keepdims=True),
        jnp.sum(grad_out, axis=0, keepdims=True),
    )


def swish_slope(values):
    logistic = jax.nn.sigmoid(values)
    return logistic * (1.0 + values * (1.0 - logistic))


def split_halves(local):
    odd = lax.axis_index("mp") % 2
    first = lax.dynamic_index_in_dim(local, odd, 0, keepdims=False)
    second = lax.dynamic_index_in_dim(local, 1 - odd, 0, keepdims=False)
    return first, second


def send_halves(first, second):
    count = lax.axis_size("mp")
    group = count // 2
    straight = [(i, i // 2 + (group if i % 2 else 0)) for i in range(count)]
    crossed = [(i, i // 2 + (0 if i % 2 else group)) for i in range(count)]
    return lax.ppermute(first, "mp", straight), lax.ppermute(second, "mp", crossed)


def join_halves(got_a, got_b):
    low_half = lax.axis_index("mp") < lax.axis_size("mp") // 2
    lower = jnp.where(low_half, got_a, got_b)
    upper = jnp.where(low_half, got_b, got_a)
    return jnp.concatenate([lower, upper], axis=0)


def send_back_parts(rows):
    half = lax.axis_index("mp") // (lax.axis_size("mp") // 2)
    frames = rows.shape[0] // 2
    lower, upper = rows[:frames], rows[frames:]
    return jnp.where(half == 0, lower, upper), jnp.where(half == 0, upper, lower)


def send_straight(rows):
    count = lax.axis_size("mp")
    group = count // 2
    return lax.ppermute(
        rows, "mp", [(i // 2 + (group if i % 2 else 0), i) for i in range(count)]
    )


def send_crossed(rows):
    count = lax.axis_size("mp")
    group = count // 2
    return lax.ppermute(
        rows, "mp", [(i // 2 + (0 if i % 2 else group), i) for i in range(count)]
    )


def send_back(rows):
    first, second = send_back_parts(rows)
    return send_straight(first), send_crossed(second)


def join_back(got_a, got_b):
    even = lax.axis_index("mp") % 2 == 0
    return jnp.stack([jnp.where(even, got_a, got_b), jnp.where(even, got_b, got_a)]).astype(F32)


hold = lax.optimization_barrier


def rounds_fit():
    return lax.axis_size("dp") == 4 and lax.axis_size("mp") == 8


def add_rounded(one, two):
    return (one.astype(F32) + two.astype(F32)).astype(BF)


def reordered(parts, index):
    count = parts.shape[0]
    return jnp.concatenate(
        [lax.dynamic_slice_in_dim(parts, k ^ index, 1, axis=0) for k in range(count)], axis=0
    )


def joined_z(parts):
    stacked = jnp.stack([parts[r] for r in sorted(parts)])
    ordered = jnp.moveaxis(reordered(stacked, lax.axis_index("mp") // 2), 0, 1)
    return ordered.reshape(-1, *ordered.shape[2:])


def spread_z(piece):
    parts = {0: piece}
    for bit in reversed(bits_of(lax.axis_size("mp"))[1:]):
        for index in list(parts):
            parts[index | bit] = swap(parts[index], "mp", bit)
    return parts


def spread_dp(pair):
    count = lax.axis_size("dp")
    if count != 4:
        for bit in bits_of(count):
            pair = jnp.concatenate([pair, swap(pair, "dp", bit)], axis=1)
        return pair
    by_x, by_y = hold((swap(pair, "dp", 1), swap(pair, "dp", 2)))
    both = jnp.stack([swap(by_y[0], "dp", 1), swap(by_x[1], "dp", 2)])
    return jnp.concatenate([pair, by_x, by_y, both], axis=1)


def spread_small(small):
    for bit in bits_of(lax.axis_size("mp")):
        small = jnp.concatenate([small, swap(small, "mp", bit)], axis=0)
    return small


def spread_rounds(piece, small, middle, late, halves, far_weight, counts):
    far_bit = lax.axis_size("mp") // 2
    if not rounds_fit():
        parts = spread_z(piece)
        near, far = (
            spread_dp(
                jnp.concatenate([parts[r] for r in sorted(parts) if (r & far_bit) == want], axis=1)
            )
            for want in (0, far_bit)
        )
        blocks = (near, swap(near, "mp", 1), far, swap(far, "mp", 1))
        return (
            blocks,
            spread_small(small[None]),
            joined_z(spread_z(middle)),
            joined_z(spread_z(late)),
            send_halves(*halves),
            swap(far_weight, "mp", far_bit),
            counts,
        )
    small = jnp.stack([small, swap(small, "mp", 1)])
    near, far, halves, got, counts, middle, late = hold(
        (
            swap(piece, "mp", 2),
            swap(piece, "mp", 4),
            halves,
            swap(small, "mp", 2),
            counts,
            middle,
            late,
        )
    )
    small = jnp.concatenate([small, got], axis=0)
    part_a = jnp.concatenate([piece, near], axis=1)
    a_x, a_y, far_near, far_weight, small, halves = hold(
        (
            swap(part_a, "dp", 1),
            swap(part_a, "dp", 2),
            swap(far, "mp", 2),
            far_weight,
            small,
            send_halves(*halves),
        )
    )
    part_b = jnp.concatenate([far, far_near], axis=1)
    ahead = jnp.concatenate([middle.reshape(2, -1, middle.shape[-1]), late], axis=1)
    b_x, b_y, a_0, a_1, far_weight, ahead = hold(
        (
            swap(part_b, "dp", 1),
            swap(part_b, "dp", 2),
            swap(a_y[0], "dp", 1),
            swap(a_x[1], "dp", 2),
            swap(far_weight, "mp", 4),
            ahead,
        )
    )
    all_a = jnp.concatenate([part_a, a_x, a_y, jnp.stack([a_0, a_1])], axis=1)
    b_0, b_1, other_a, ahead_near, mid_far, got = hold(
        (
            swap(b_y[0], "dp", 1),
            swap(b_x[1], "dp", 2),
            swap(all_a, "mp", 1),
            swap(ahead, "mp", 2),
            swap(middle, "mp", 4),
            swap(small, "mp", 4),
        )
    )
    small = jnp.concatenate([small, got], axis=0)
    cut = ahead.shape[1] - late.shape[1]
    all_b = jnp.concatenate([part_b, b_x, b_y, jnp.stack([b_0, b_1])], axis=1)
    return (
        (all_a, other_a, all_b, swap(all_b, "mp", 1)),
        small,
        {0: middle, 2: ahead_near[:, :cut].reshape(middle.shape), 4: mid_far},
        {0: late, 2: ahead_near[:, cut:]},
        halves,
        far_weight,
        counts,
    )


def z_groups():
    count = lax.axis_size("mp")
    return [list(range(core, count, 2)) for core in range(2)]


def collect_z_relative(parts):
    live = {2 * k: parts[k] for k in range(parts.shape[0])}
    for bit in bits_of(lax.axis_size("mp"))[1:]:
        for index in [r for r in live if r & bit]:
            live[index ^ bit] = add_rounded(live[index ^ bit], swap(live.pop(index), "mp", bit))
    return live[0]


def halve_z(parts, bit):
    return add_rounded(parts[0::2], swap(parts[1::2], "mp", bit))


def collect_dp(pair):
    for bit in reversed(bits_of(lax.axis_size("dp"))):
        rows = pair.shape[1] // 2
        pair = add_rounded(pair[:, :rows], swap(pair[:, rows:], "dp", bit))
    return pair


def corners(parts):
    half = parts[3].shape[0] // 2
    return swap(parts[3][:half], "dp", 1), swap(parts[3][half:], "dp", 2)


def sides(parts, to_x, to_y):
    half = parts[0].shape[0] // 2
    via_x = jnp.concatenate([parts[1][:half], add_rounded(parts[1][half:], to_y)], axis=0)
    via_y = jnp.concatenate([add_rounded(parts[2][:half], to_x), parts[2][half:]], axis=0)
    return swap(via_x, "dp", 1), swap(via_y, "dp", 2)


def finish(parts, got_x, got_y):
    return (parts[0].astype(F32) + got_x.astype(F32) + got_y.astype(F32)).astype(BF)


def collect_plain(grads_in, grads_out, z_parts, far_part):
    far_bit = lax.axis_size("mp") // 2
    sums = []
    for far in (0, 1):
        own, other = (jnp.stack([grads_in[2 * far + k], grads_out[2 * far + k]]) for k in range(2))
        sums.append(collect_dp(add_rounded(own, swap(other, "mp", 1))))
    count = lax.axis_size("mp") // 4
    stacked = jnp.concatenate([jnp.stack(jnp.split(part, count, axis=1)) for part in sums], axis=0)
    own = collect_z_relative(stacked)
    own = jnp.concatenate(
        [
            own.reshape(-1, own.shape[-1]),
            collect_z_relative(z_parts),
            add_rounded(far_part[0], swap(far_part[1], "mp", far_bit)),
        ],
        axis=0,
    )
    for bit in bits_of(lax.axis_size("dp")):
        own = jnp.concatenate([own, swap(own, "dp", bit)], axis=0)
    return own.reshape(lax.axis_size("dp"), -1, own.shape[-1])


def combine_everywhere(rows, combine, beside=None):
    order = [("mp", bit) for bit in bits_of(lax.axis_size("mp"))]
    order[1:1] = [("dp", bit) for bit in bits_of(lax.axis_size("dp"))]
    for step, (axis, bit) in enumerate(order):
        got = swap(rows, axis, bit)
        if beside is not None and step < len(beside) and beside[step] is not None:
            got, beside[step] = hold((got, beside[step]))
        rows = combine(rows, got)
    return rows


def ffn_forward(resid, gain_vec, shift_vec, blocks, b_out, beside=None):
    normed, unit_rows, inv_scale = norm_forward(resid, gain_vec, shift_vec)
    act = normed.astype(BF)
    branch = b_out
    uppers, hiddens = [], []
    for w_in_t, w_out, b_in in blocks:
        upper = dot_nt(act, w_in_t) + b_in
        hidden = jax.nn.silu(upper).astype(BF)
        branch = branch + dot_nn(hidden, w_out)
        uppers.append(upper)
        hiddens.append(hidden)
        if beside is not None and 2 * len(uppers) == len(blocks):
            branch, beside[0] = hold((branch, beside[0]))
    return branch, (unit_rows, inv_scale, act, uppers, hiddens)


def block_backward(grad_branch, act, block, upper, hidden):
    w_in_t, w_out, _ = block
    grad_hidden = dot_nt(grad_branch, w_out)
    grad_upper = (grad_hidden * swish_slope(upper)).astype(BF)
    return (
        dot_nn(grad_upper, w_in_t),
        dot_tn(grad_upper, act).astype(BF),
        dot_tn(hidden, grad_branch).astype(BF),
        jnp.sum(grad_upper, axis=0, dtype=F32, keepdims=True),
    )


def ffn_backward(grad_resid, saved, gain_vec, blocks, between=None):
    unit_rows, inv_scale, act, uppers, hiddens = saved
    grad_branch = (0.5 * grad_resid).astype(BF)
    grad_b_out = jnp.sum(grad_branch, axis=0, dtype=F32, keepdims=True)
    grad_act = 0.0
    count = len(blocks)
    grads_in, grads_out, grads_b = [None] * count, [None] * count, [None] * count
    for k in reversed(range(count)):
        part, grads_in[k], grads_out[k], grads_b[k] = block_backward(
            grad_branch, act, blocks[k], uppers[k], hiddens[k]
        )
        grad_act = grad_act + part
        if between is not None:
            grad_act, grad_branch, grads_in[k], grads_out[k] = between(
                k, (grad_act, grad_branch, grads_in[k], grads_out[k])
            )
    grad_in, grad_gain, grad_shift = norm_backward(grad_act, unit_rows, inv_scale, gain_vec)
    return (
        grad_resid + grad_in,
        (grads_in, grads_b, grads_out),
        (grad_gain, grad_shift, grad_b_out),
    )


def pair_mask(shape, head):
    lane = lax.broadcasted_iota(jnp.int32, shape, len(shape) - 1)
    return (lane // HEAD) == head


def attend_kernel(q_ref, k_ref, v_ref, bias_ref, out_ref, wide_ref, lse_ref):
    query, key, value = q_ref[...], k_ref[...], v_ref[...]
    bias = bias_ref[...]
    factor = LOG2E / math.sqrt(HEAD)
    mixed, logs = [], []
    for head in range(2):
        masked = jnp.where(pair_mask(query.shape, head), query, jnp.zeros_like(query))
        scores = dot_nt(masked, key) * factor + bias
        row_max = jnp.max(scores, axis=-1, keepdims=True)
        shifted = jnp.exp2(scores - row_max)
        total = jnp.sum(shifted, axis=-1, keepdims=True)
        mixed.append(dot_nn(shifted.astype(BF), value) * (1.0 / total))
        logs.append(row_max + jnp.log2(total))
    first = pair_mask(mixed[0].shape, 0)
    wide = jnp.where(first, mixed[0], mixed[1])
    wide_ref[...] = wide
    out_ref[...] = wide.astype(BF)
    lse_ref[...] = jnp.where(first, logs[0], logs[1])


def attend_forward(query, key, value, bias, block):
    frames, columns = query.shape
    pairs = columns // (2 * HEAD)
    rows_spec = pl.BlockSpec((block, 2 * HEAD), lambda p, i: (i, p))
    whole_spec = pl.BlockSpec((frames, 2 * HEAD), lambda p, i: (0, p))
    return pl.pallas_call(
        attend_kernel,
        grid=(pairs, frames // block),
        in_specs=[rows_spec, whole_spec, whole_spec, pl.BlockSpec((1, frames), lambda p, i: (0, 0))],
        out_specs=[rows_spec, rows_spec, rows_spec],
        out_shape=[
            jax.ShapeDtypeStruct((frames, columns), BF),
            jax.ShapeDtypeStruct((frames, columns), F32),
            jax.ShapeDtypeStruct((frames, columns), F32),
        ],
        compiler_params=pltpu.CompilerParams(vmem_limit_bytes=56 * 1024 * 1024),
        cost_estimate=pl.CostEstimate(
            flops=8 * frames * frames * columns,
            bytes_accessed=12 * frames * columns,
            transcendentals=frames * frames * columns // HEAD,
        ),
        name="attend_forward",
    )(query, key, value, bias)


def attend_back_kernel(
    q_ref, k_ref, v_ref, g_ref, wide_ref, lse_ref, bias_ref, dq_ref, dk_ref, dv_ref, dk_acc, dv_acc
):
    step = pl.program_id(1)
    query, key, value, grad = q_ref[...], k_ref[...], v_ref[...], g_ref[...]
    bias = bias_ref[...]
    lse = lse_ref[...]
    factor = LOG2E / math.sqrt(HEAD)
    scale = 1.0 / math.sqrt(HEAD)
    both = grad.astype(F32) * wide_ref[...]
    dq, new_dk, new_dv = [], 0.0, 0.0
    for head in range(2):
        mask = pair_mask(query.shape, head)
        query_h = jnp.where(mask, query, jnp.zeros_like(query))
        grad_h = jnp.where(mask, grad, jnp.zeros_like(grad))
        scores = dot_nt(query_h, key) * factor + bias
        probs = jnp.exp2(scores - lse[:, head * HEAD : head * HEAD + 1])
        grad_probs = dot_nt(grad_h, value)
        row_dot = jnp.sum(jnp.where(mask, both, 0.0), axis=-1, keepdims=True)
        grad_scores = (probs * (grad_probs - row_dot)).astype(BF)
        new_dv = new_dv + dot_tn(grad_h, probs.astype(BF))
        dq.append(dot_nn(grad_scores, key))
        new_dk = new_dk + dot_tn(query_h, grad_scores)
    first = pair_mask(dq[0].shape, 0)
    dq_ref[...] = (jnp.where(first, dq[0], dq[1]) * scale).astype(BF)

    @pl.when(step == 0)
    def _():
        dk_acc[...] = new_dk
        dv_acc[...] = new_dv

    @pl.when(step > 0)
    def _():
        dk_acc[...] += new_dk
        dv_acc[...] += new_dv

    @pl.when(step == pl.num_programs(1) - 1)
    def _():
        dk_ref[...] = (dk_acc[...] * scale).T.astype(BF)
        dv_ref[...] = dv_acc[...].T.astype(BF)


def attend_backward(query, key, value, grad, wide, lse, bias, block):
    frames, columns = query.shape
    pairs = columns // (2 * HEAD)
    rows_spec = pl.BlockSpec((block, 2 * HEAD), lambda p, i: (i, p))
    whole_spec = pl.BlockSpec((frames, 2 * HEAD), lambda p, i: (0, p))
    shape = jax.ShapeDtypeStruct((frames, columns), BF)
    return pl.pallas_call(
        attend_back_kernel,
        grid=(pairs, frames // block),
        in_specs=[
            rows_spec,
            whole_spec,
            whole_spec,
            rows_spec,
            rows_spec,
            rows_spec,
            pl.BlockSpec((1, frames), lambda p, i: (0, 0)),
        ],
        out_specs=[rows_spec, whole_spec, whole_spec],
        out_shape=[shape, shape, shape],
        scratch_shapes=[
            pltpu.VMEM((2 * HEAD, frames), F32),
            pltpu.VMEM((2 * HEAD, frames), F32),
        ],
        compiler_params=pltpu.CompilerParams(vmem_limit_bytes=56 * 1024 * 1024),
        cost_estimate=pl.CostEstimate(
            flops=20 * frames * frames * columns,
            bytes_accessed=20 * frames * columns,
            transcendentals=frames * frames * columns // HEAD,
        ),
        name="attend_backward",
    )(query, key, value, grad, wide, lse, bias)


def add_parts_kernel(one_ref, got_one_ref, two_ref, got_two_ref, out_ref):
    out_ref[0] = (one_ref[...].astype(F32) + got_one_ref[...].astype(F32)).astype(BF)
    out_ref[1] = (two_ref[...].astype(F32) + got_two_ref[...].astype(F32)).astype(BF)


def add_parts(one, got_one, two, got_two, parts):
    rows, width = one.shape
    part = rows // parts
    step = math.gcd(part, 256)
    steps = part // step
    spec = pl.BlockSpec((step, width), lambda p, j: (p * steps + j, 0))
    return pl.pallas_call(
        add_parts_kernel,
        grid=(parts, steps),
        in_specs=[spec] * 4,
        out_specs=pl.BlockSpec((None, 2, step, width), lambda p, j: (p, 0, j, 0)),
        out_shape=jax.ShapeDtypeStruct((parts, 2, part, width), BF),
        compiler_params=pltpu.CompilerParams(vmem_limit_bytes=32 * 1024 * 1024),
        cost_estimate=pl.CostEstimate(
            flops=2 * rows * width, bytes_accessed=12 * rows * width, transcendentals=0
        ),
        name="add_parts",
    )(one, got_one, two, got_two)


def unpack_kernel(index_ref, part_ref, in_ref, out_ref):
    rows = out_ref.shape[0]
    in_ref[...] = part_ref[:rows].astype(F32).T
    out_ref[...] = part_ref[rows:].astype(F32)


def unpack(parts, index, rows, place):
    count, _, width = parts.shape
    return pl.pallas_call(
        unpack_kernel,
        grid_spec=pltpu.PrefetchScalarGridSpec(
            num_scalar_prefetch=1,
            grid=(count,),
            in_specs=[
                pl.BlockSpec((None, 2 * rows, width), lambda r, at: (r, place // (2 * rows), 0))
            ],
            out_specs=[
                pl.BlockSpec((width, rows), lambda r, at: (0, at[0] ^ r)),
                pl.BlockSpec((rows, width), lambda r, at: (at[0] ^ r, 0)),
            ],
        ),
        out_shape=[
            jax.ShapeDtypeStruct((width, count * rows), F32),
            jax.ShapeDtypeStruct((count * rows, width), F32),
        ],
        compiler_params=pltpu.CompilerParams(vmem_limit_bytes=32 * 1024 * 1024),
        cost_estimate=pl.CostEstimate(
            flops=0, bytes_accessed=12 * count * rows * width, transcendentals=0
        ),
        name="unpack",
    )(index.reshape(1), parts)


def lay_out(buffer, before, rows, after, halo):
    count = rows.shape[0]
    buffer[:halo] = before[...]
    buffer[halo : halo + count] = rows[...]
    buffer[halo + count :] = after[...]


def depth_kernel(
    before_ref, rows_ref, after_ref, taps_ref, visible_ref, depth_ref, stats_ref, padded, *, taps
):
    count, lanes = depth_ref.shape
    halo = before_ref.shape[0]
    first = halo - taps // 2
    lay_out(padded, before_ref, rows_ref, after_ref, halo)
    depth = jnp.zeros((count, lanes), F32)
    for phase in range(8):
        more = (taps - 1 - phase) // 8
        base = padded[first + phase : first + phase + count + 8 * more]
        for step in range(more + 1):
            tap = 8 * step + phase
            depth = depth + base[8 * step : 8 * step + count] * taps_ref[tap : tap + 1]
    depth_ref[...] = depth
    visible = visible_ref[...]
    frames = jnp.sum(visible, axis=0, keepdims=True)
    mean = jnp.sum(depth * visible, axis=0, keepdims=True) / jnp.maximum(frames, 1.0)
    apart = (depth - mean) * visible
    stats_ref[0:1] = jnp.broadcast_to(frames, (1, lanes))
    stats_ref[1:2] = mean
    stats_ref[2:3] = jnp.sum(apart * apart, axis=0, keepdims=True)
    stats_ref[3:] = jnp.zeros((5, lanes), F32)


def depth_forward(rows, around, taps_rows, visible, taps):
    count, width = rows.shape
    lanes = 128
    halo = around[0].shape[0]

    def column(height):
        return pl.BlockSpec((height, lanes), lambda j: (0, j))

    return pl.pallas_call(
        functools.partial(depth_kernel, taps=taps),
        grid=(width // lanes,),
        in_specs=[
            column(halo),
            column(count),
            column(halo),
            column(taps_rows.shape[0]),
            pl.BlockSpec((count, 1), lambda j: (0, 0)),
        ],
        out_specs=[column(count), column(8)],
        out_shape=[
            jax.ShapeDtypeStruct((count, width), F32),
            jax.ShapeDtypeStruct((8, width), F32),
        ],
        scratch_shapes=[pltpu.VMEM((count + 2 * halo, lanes), F32)],
        cost_estimate=pl.CostEstimate(
            flops=2 * taps * count * width, bytes_accessed=9 * count * width, transcendentals=0
        ),
        name="depth_forward",
    )(around[0], rows, around[1], taps_rows, visible)


def depth_back_kernel(
    gbefore_ref,
    grad_ref,
    gafter_ref,
    before_ref,
    rows_ref,
    after_ref,
    taps_ref,
    visible_ref,
    value_ref,
    logistic_ref,
    gvalue_ref,
    ggate_ref,
    gtaps_ref,
    gbias_ref,
    gpadded,
    padded,
    *,
    taps,
):
    count, lanes = grad_ref.shape
    halo = before_ref.shape[0]
    first = halo - taps // 2
    lay_out(gpadded, gbefore_ref, grad_ref, gafter_ref, halo)
    lay_out(padded, before_ref, rows_ref, after_ref, halo)
    tap_rows = taps_ref[...]
    sums = [jnp.zeros((8, lanes), F32) for _ in range(taps)]
    tile = math.gcd(count, 32)
    gvalue, ggate = 0.0, 0.0
    for start in range(0, count, tile):
        here = slice(start, start + tile)
        grad = grad_ref[here]
        total = jnp.zeros((tile, lanes), F32)
        for tap in range(taps):
            there = slice(first + start + tap, first + start + tap + tile)
            total = total + gpadded[there] * tap_rows[taps - 1 - tap : taps - tap]
            product = (grad * padded[there]).reshape(tile // 8, 8, lanes)
            sums[tap] = sums[tap] + jnp.sum(product, axis=0)
        grad_gated = total * visible_ref[here]
        logistic = logistic_ref[here]
        value_part = (grad_gated * logistic).astype(BF)
        gate_part = (grad_gated * value_ref[here] * logistic * (1.0 - logistic)).astype(BF)
        gvalue_ref[here] = value_part
        ggate_ref[here] = gate_part
        gvalue = gvalue + jnp.sum(value_part.astype(F32), axis=0, keepdims=True)
        ggate = ggate + jnp.sum(gate_part.astype(F32), axis=0, keepdims=True)
    for tap in range(taps):
        gtaps_ref[tap : tap + 1] = jnp.sum(sums[tap], axis=0, keepdims=True)
    gbias_ref[0:1] = gvalue
    gbias_ref[1:2] = ggate
    gbias_ref[2:] = jnp.zeros((6, lanes), F32)


def depth_backward(grad, garound, rows, around, taps_rows, visible, value, logistic, taps):
    count, width = rows.shape
    lanes = 128
    halo = around[0].shape[0]

    def column(height):
        return pl.BlockSpec((height, lanes), lambda j: (0, j))

    return pl.pallas_call(
        functools.partial(depth_back_kernel, taps=taps),
        grid=(width // lanes,),
        in_specs=[
            column(halo),
            column(count),
            column(halo),
            column(halo),
            column(count),
            column(halo),
            column(taps_rows.shape[0]),
            pl.BlockSpec((count, 1), lambda j: (0, 0)),
            column(count),
            column(count),
        ],
        out_specs=[column(count), column(count), column(taps_rows.shape[0]), column(8)],
        out_shape=[
            jax.ShapeDtypeStruct((count, width), BF),
            jax.ShapeDtypeStruct((count, width), BF),
            jax.ShapeDtypeStruct(taps_rows.shape, F32),
            jax.ShapeDtypeStruct((8, width), F32),
        ],
        scratch_shapes=[pltpu.VMEM((count + 2 * halo, lanes), F32)] * 2,
        cost_estimate=pl.CostEstimate(
            flops=4 * taps * count * width, bytes_accessed=24 * count * width, transcendentals=0
        ),
        name="depth_backward",
    )(
        garound[0], grad, garound[1], around[0], rows, around[1], taps_rows, visible, value, logistic
    )


def spread_blocks(local, group):
    blocks = {0: local}
    for bit in reversed(bits_of(group)):
        for index in list(blocks):
            blocks[index | bit] = swap(blocks[index], "mp", bit)
    return [blocks[r] for r in range(group)]


def collect_blocks(parts):
    live = dict(enumerate(parts))
    for bit in bits_of(len(parts)):
        for index in [r for r in live if not r & bit]:
            sent = swap(live.pop(index | bit).astype(BF), "mp", bit)
            live[index] = live[index] + sent.astype(F32)
    return live[0]


def exchange_blocks(parts):
    return [parts[0]] + [swap(parts[r], "mp", r) for r in range(1, len(parts))]


def shards(
    frames,
    lengths,
    mask_flags,
    mask_embed,
    ffa_gain,
    ffa_shift,
    ffa_w_in,
    ffa_b_in,
    ffa_w_out,
    ffa_b_out,
    att_gain,
    att_shift,
    att_w_qkv,
    att_b_qv,
    att_w_out,
    att_b_out,
    conv_gain,
    conv_shift,
    conv_w_in,
    conv_b_in,
    conv_w_depth,
    batch_scale,
    batch_shift,
    running_mean,
    running_var,
    conv_w_out,
    conv_b_out,
    ffb_gain,
    ffb_shift,
    ffb_w_in,
    ffb_b_in,
    ffb_w_out,
    ffb_b_out,
    final_gain,
    final_shift,
    cotangent,
):
    mask_embed = mask_embed[None]
    ffa_gain = ffa_gain[None]
    ffa_shift = ffa_shift[None]
    ffa_b_out = ffa_b_out[None]
    att_gain = att_gain[None]
    att_shift = att_shift[None]
    att_b_out = att_b_out[None]
    conv_gain = conv_gain[None]
    conv_shift = conv_shift[None]
    conv_b_out = conv_b_out[None]
    ffb_gain = ffb_gain[None]
    ffb_shift = ffb_shift[None]
    ffb_b_out = ffb_b_out[None]
    final_gain = final_gain[None]
    final_shift = final_shift[None]
    dp = lax.axis_size("dp")
    mp = lax.axis_size("mp")
    zs = mp // 2
    group = mp // 2
    d = lax.axis_index("dp")
    m = lax.axis_index("mp")
    core = m % 2
    half = m // group
    q = m % group
    width = frames.shape[2]
    columns = width // mp
    rows_local = 2 * mask_flags.shape[1]
    hidden_q = ffa_b_in.shape[0] // dp
    chan_q = columns // dp
    taps = conv_w_depth.shape[0]
    reach = taps // 2

    small = jnp.concatenate(
        [
            ffa_b_in.astype(F32).reshape(-1, columns),
            ffb_b_in.astype(F32).reshape(-1, columns),
            conv_b_in,
            conv_w_depth,
            batch_scale[None],
            batch_shift[None],
            att_b_qv,
        ],
        axis=0,
    )
    low = mp // 4

    def relative_bias(far, near_core):
        first = far * (mp // 2) + near_core
        part = bias_rel[first : first + 2 * low : 2]
        return part.transpose(1, 0, 2).reshape(1, -1)


    def hidden_bias(rows):
        both = rows.reshape(zs, 2, dp * hidden_q).transpose(1, 0, 2).reshape(2, -1)
        own = lax.dynamic_slice_in_dim(both, core, 1, axis=0)
        other = lax.dynamic_slice_in_dim(both, 1 - core, 1, axis=0)
        return own, other

    def to_canon(rows):
        lead = rows.shape[:-1]
        split = rows.reshape(*lead, zs, 2, columns)
        return jnp.moveaxis(split, -3, -2).reshape(*lead, width)

    def from_canon(rows):
        lead = rows.shape[:-1]
        split = rows.reshape(*lead, 2, zs, columns)
        return jnp.moveaxis(split, -3, -2).reshape(*lead, width)

    def own_columns(rows):
        return lax.dynamic_slice_in_dim(rows, m * columns, columns, axis=-1)

    def hidden_pieces(w_in, w_out):
        piece_in = lax.dynamic_slice_in_dim(w_in, d * hidden_q, hidden_q, axis=1).T
        piece_out = lax.dynamic_slice_in_dim(w_out, d * hidden_q, hidden_q, axis=0)
        return piece_in, piece_out

    def channel_piece(rows):
        return lax.dynamic_slice_in_dim(rows, d * chan_q, chan_q, axis=0)

    kinds = [conv_w_in[0].T, conv_w_in[1].T, conv_w_out, att_w_out]
    valid_count = jnp.sum(lengths).astype(F32)
    for bit in bits_of(dp):
        valid_count = valid_count + swap(valid_count, "dp", bit)
    flags = jnp.pad(mask_flags.astype(BF), ((0, 0), (0, 16 * width - mask_flags.shape[1])))
    frames = jnp.concatenate([frames, flags.reshape(2, 16, width)], axis=1)
    per = ffa_b_in.shape[0] // columns
    gathered, small, mid_z, late_z, halves, w_other, valid_count = spread_rounds(
        jnp.stack(hidden_pieces(ffa_w_in, ffa_w_out)),
        jnp.pad(small, ((0, -small.shape[0] % 16), (0, 0))).reshape(-1, width),
        jnp.stack([channel_piece(rows) for rows in kinds]),
        jnp.stack(hidden_pieces(ffb_w_in, ffb_w_out)),
        split_halves(frames),
        att_w_qkv,
        valid_count,
    )
    small = small.reshape(mp, -1, columns)[:, : 2 * per + 6 + taps]
    bias_rel = small[:, :per].reshape(mp, dp, hidden_q)[:, jnp.arange(dp) ^ d]
    small = small[jnp.arange(mp) ^ m]
    bias_b = hidden_bias(small[:, per : 2 * per])
    small = small[:, 2 * per :]
    conv_small = to_canon(jnp.moveaxis(small[:, : 4 + taps], 0, 1).reshape(-1, width))
    b_qv = jnp.moveaxis(small[:, 4 + taps :], 0, 1).reshape(2, 2, group, columns)
    b_qv = lax.dynamic_index_in_dim(b_qv, q, 2, keepdims=False).reshape(2, -1)
    frames_local = mask_flags.shape[1]
    rows_in = join_halves(*(part[:frames_local] for part in halves))
    flag_rows = [part[frames_local:].reshape(-1)[:frames_local, None] for part in halves]
    flag_rows = join_halves(*flag_rows).astype(F32)
    c_b_in = [conv_small[0:1], conv_small[1:2]]
    c_depth = jnp.pad(conv_small[2 : 2 + taps], ((0, -taps % 8), (0, 0)))
    c_scale = conv_small[2 + taps : 3 + taps]
    c_shift = conv_small[3 + taps : 4 + taps]
    blocks_a = [
        (gathered[k][0], gathered[k][1], relative_bias(k // 2, k % 2)) for k in range(4)
    ]
    if not rounds_fit():
        mid_own = lax.all_gather(mid_z, "dp", axis=1, tiled=True)
        late_own = lax.all_gather(late_z, "dp", axis=1, tiled=True)

    length = lax.dynamic_index_in_dim(lengths, half, 0, keepdims=False)
    place = q * rows_local + jnp.arange(rows_local)
    visible = (place < length).astype(F32)[:, None]
    key_place = ((jnp.arange(group) ^ q)[:, None] * rows_local + jnp.arange(rows_local)).reshape(1, -1)
    key_bias = jnp.where(key_place < length, 0.0, -1e30).astype(F32)

    resid_a = rows_in.astype(F32) + flag_rows * mask_embed
    if rounds_fit():
        beside = [swap(mid_z[4], "mp", 2)]
        branch, saved_a = ffn_forward(resid_a, ffa_gain, ffa_shift, blocks_a, ffa_b_out, beside)
        mid_z = joined_z({**mid_z, 6: beside[0]})
        mid_own = lax.all_gather(mid_z, "dp", axis=1, tiled=True)
    else:
        branch, saved_a = ffn_forward(resid_a, ffa_gain, ffa_shift, blocks_a, ffa_b_out)
    resid_b = resid_a + 0.5 * branch

    normed, att_unit, att_inv = norm_forward(resid_b, att_gain, att_shift)
    att_act = normed.astype(BF)
    if rounds_fit():
        near, by_core_act, late_far = hold(
            (swap(att_act, "mp", 2), swap(att_act, "mp", 1), swap(late_z[0], "mp", 4))
        )
        blocks = [att_act, by_core_act, near, swap(near, "mp", 1)]
    else:
        blocks = spread_blocks(att_act, group)
    w_qkv = jnp.concatenate(
        [jnp.where(half == 0, att_w_qkv, w_other), jnp.where(half == 0, w_other, att_w_qkv)], axis=2
    )
    att_rows = jnp.concatenate(blocks, axis=0)
    query = (dot_nn(att_rows, w_qkv[0]) + b_qv[0]).astype(BF)
    key = dot_nn(att_rows, w_qkv[1]).astype(BF)
    value = (dot_nn(att_rows, w_qkv[2]) + b_qv[1]).astype(BF)
    if rounds_fit():
        query, key, value, late_both, mid_own = hold(
            (query, key, value, swap(late_far, "mp", 2), mid_own)
        )
        late_z = joined_z({**late_z, 4: late_far, 6: late_both})
        late_own = lax.all_gather(late_z, "dp", axis=1, tiled=True)
    block = group * rows_local // 2
    mixed_cols, mixed_wide, lse = attend_forward(query, key, value, key_bias, block)
    mid_other = swap(mid_own, "mp", 1)
    parts = [mixed_cols[r * rows_local : (r + 1) * rows_local] for r in range(group)]
    parts = exchange_blocks(parts)
    mid = jnp.stack(
        [
            jnp.where(core == 0, one, two).reshape(4, zs, columns, width)
            for one, two in ((mid_own, mid_other), (mid_other, mid_own))
        ],
        axis=1,
    )
    conv_value_w, conv_gate_w, conv_out_w = (mid[k].reshape(width, width) for k in range(3))
    att_out_w = mid[3].transpose(1, 0, 2, 3).reshape(2, group, columns, width)
    att_out_w = reordered(jnp.moveaxis(att_out_w, 1, 0), q).reshape(width, width)
    *parts, conv_value_w, conv_gate_w, conv_out_w, att_out_w, cotangent = hold(
        (*parts, conv_value_w, conv_gate_w, conv_out_w, att_out_w, cotangent)
    )
    cot_halves = send_halves(*split_halves(cotangent))
    mixed = jnp.concatenate(parts, axis=1)
    resid_c = resid_b + (dot_nn(mixed, att_out_w) + att_b_out)

    normed, conv_unit, conv_inv = norm_forward(resid_c, conv_gain, conv_shift)
    conv_act = normed.astype(BF)
    pre_value = dot_nt(conv_act, conv_value_w) + c_b_in[0]
    pre_gate = dot_nt(conv_act, conv_gate_w) + c_b_in[1]
    logistic = jax.nn.sigmoid(pre_gate)
    gated = pre_value * logistic * visible

    up = [(i, i + 1) for i in range(mp - 1) if (i + 1) % group]
    down = [(i + 1, i) for i, _ in up]

    halo = -(-reach // 8) * 8

    def halos(rows):
        return lax.ppermute(rows[-halo:], "mp", up), lax.ppermute(rows[:halo], "mp", down)

    gated_halos = halos(gated)
    depth, stats = depth_forward(gated, gated_halos, c_depth, visible, taps)
    depth, stats, *cot_halves = hold((depth, stats, *cot_halves))
    cot_rows = join_halves(*cot_halves)

    def join(one, two):
        both = jnp.maximum(one[0:1] + two[0:1], 1.0)
        gap = one[1:2] - two[1:2]
        return jnp.concatenate(
            [
                one[0:1] + two[0:1],
                (one[0:1] * one[1:2] + two[0:1] * two[1:2]) / both,
                one[2:3] + two[2:3] + gap * gap * (one[0:1] * two[0:1] / both),
                one[3:],
            ],
            axis=0,
        )

    beside = [None, None, None, None, late_own]
    stats = combine_everywhere(stats, join, beside)
    late_own = beside[4].reshape(2, -1, width)
    late_other = swap(late_own, "mp", 1)
    blocks_b = [(late_own[0], late_own[1], bias_b[0]), (late_other[0], late_other[1], bias_b[1])]
    batch_mean = stats[1:2]
    batch_var = stats[2:3] / valid_count
    inv_batch = lax.rsqrt(batch_var + EPS)
    centred = depth - batch_mean
    normed_bn = centred * inv_batch * c_scale + c_shift
    swished = jax.nn.silu(normed_bn).astype(BF)
    resid_d = resid_c + (dot_nn(swished, conv_out_w) + conv_b_out)

    branch, saved_b = ffn_forward(resid_d, ffb_gain, ffb_shift, blocks_b, ffb_b_out)
    resid_e = resid_d + 0.5 * branch
    layer_rows, unit_out, inv_out = norm_forward(resid_e, final_gain, final_shift)

    grad_resid, g_final_gain, g_final_shift = norm_backward(
        cot_rows.astype(F32), unit_out, inv_out, final_gain
    )
    grad_resid, mats_b, vecs_b = ffn_backward(grad_resid, saved_b, ffb_gain, blocks_b)

    def by_core(rows):
        part = width // 2
        return [
            lax.dynamic_slice_in_dim(rows, which * part, part, axis=1) for which in (core, 1 - core)
        ]

    grad_branch = grad_resid.astype(BF)
    g_conv_b_out = jnp.sum(grad_branch, axis=0, dtype=F32, keepdims=True)
    grad_normed = dot_nt(grad_branch, conv_out_w) * swish_slope(normed_bn)
    g_conv_out = [dot_tn(rows, grad_branch).astype(BF) for rows in by_core(swished)]
    sums = jnp.concatenate(
        [
            jnp.sum(grad_normed, axis=0, keepdims=True),
            jnp.sum(grad_normed * centred, axis=0, keepdims=True),
        ],
        axis=0,
    )
    late_g = [mats_b[0][1], mats_b[2][1], mats_b[0][0], mats_b[2][0]]
    sums = combine_everywhere(sums, jnp.add, late_g)
    late_got = [swap(grads, "mp", 1) for grads in late_g[:2]]
    sums, layer_rows = hold((sums, layer_rows.astype(BF)))
    layer_out = send_back(layer_rows)
    grad_normed, *late_got = hold((grad_normed, *late_got))
    late_sum = add_parts(late_g[2], late_got[0], late_g[3], late_got[1], 1)
    late_sum = late_sum.reshape(2 * zs, dp * hidden_q, width)
    late_sum = lax.psum_scatter(late_sum, "dp", scatter_dimension=1, tiled=True)
    inv_cube = inv_batch * inv_batch * inv_batch
    grad_depth = grad_normed * (c_scale * inv_batch) - visible * (
        (inv_batch * c_scale * sums[0:1] + inv_cube * c_scale * sums[1:2] * centred) / valid_count
    )
    grad_value_pre, grad_gate_pre, g_depth, g_conv_b_in = depth_backward(
        grad_depth,
        halos(grad_depth),
        gated,
        gated_halos,
        c_depth,
        visible,
        pre_value,
        logistic,
        taps,
    )
    grad_act = dot_nn(grad_value_pre, conv_value_w) + dot_nn(grad_gate_pre, conv_gate_w)
    g_conv_value = [dot_tn(rows, conv_act).astype(BF) for rows in by_core(grad_value_pre)]
    g_conv_gate = [dot_tn(rows, conv_act).astype(BF) for rows in by_core(grad_gate_pre)]
    grad_in, g_conv_gain, g_conv_shift = norm_backward(grad_act, conv_unit, conv_inv, conv_gain)
    grad_resid = grad_resid + grad_in

    grad_branch = grad_resid.astype(BF)
    g_att_b_out = jnp.sum(grad_branch, axis=0, dtype=F32, keepdims=True)
    grad_mixed = dot_nt(grad_branch, att_out_w).astype(BF)
    g_att_out = []
    for which in range(2):
        one = [
            lax.dynamic_slice_in_dim(
                mixed,
                ((((q // 2) ^ k) * 2 + which) * 2 + slot) * columns,
                columns,
                axis=1,
            )
            for slot in range(2)
            for k in range(group // 2)
        ]
        g_att_out.append(dot_tn(jnp.concatenate(one, axis=1), grad_branch).astype(BF))
    wide = 2 * columns
    parts = [grad_mixed[:, r * wide : (r + 1) * wide] for r in range(group)]
    grad_cols = jnp.concatenate(exchange_blocks(parts), axis=0)
    grad_q, grad_k, grad_v = attend_backward(
        query, key, value, grad_cols, mixed_wide, lse, key_bias, block
    )

    grad_q, grad_k, grad_v, late_sum = hold((grad_q, grad_k, grad_v, late_sum))
    late_sum = late_sum.reshape(2, zs, hidden_q, width)
    late_parts = reordered(jnp.moveaxis(late_sum, 1, 0).reshape(zs, -1, width), m // 2)
    if rounds_fit():
        late_got = swap(late_parts[1::2], "mp", 2)
    mid_g = [g_conv_value, g_conv_gate, g_conv_out, g_att_out]
    mid_got = swap(jnp.concatenate([g[1] for g in mid_g], axis=0), "mp", 1)
    grad_all = jnp.concatenate([grad_q, grad_k, grad_v], axis=1)
    w_flat = jnp.concatenate([w_qkv[0], w_qkv[1], w_qkv[2]], axis=1)
    partial = dot_nt(grad_all, w_flat)
    g_qkv = dot_tn(grad_all, att_rows).astype(BF)
    partial, *layer_out = hold((partial, *layer_out))
    partial = [partial[r * rows_local : (r + 1) * rows_local] for r in range(group)]
    if rounds_fit():
        got_0, got_1, mid_got = hold(
            (
                swap(partial[1].astype(BF), "mp", 1),
                swap(partial[3].astype(BF), "mp", 1),
                mid_got,
            )
        )
        to_near = (partial[2] + got_1.astype(F32)).astype(BF)
        to_near, mid_got, g_qkv = hold((to_near, mid_got, g_qkv))
    mid_got = mid_got.reshape(4, zs, columns, width)
    joint = [
        add_rounded(g[0].reshape(zs, columns, width), got)
        for g, got in zip(mid_g, mid_got, strict=True)
    ] + [g_qkv.reshape(6, columns, width)]
    joint_rows = (4 * zs + 6) * chan_q
    if rounds_fit():
        joint_parts = []
        for r in range(dp):
            part = [
                lax.dynamic_slice_in_dim(rows, (d ^ r) * chan_q, chan_q, axis=1) for rows in joint
            ]
            joint_parts.append(jnp.concatenate(part, axis=0).reshape(joint_rows, width))
        joint_corners = corners(joint_parts)
    if rounds_fit():
        got, late_got, *joint_corners = hold((swap(to_near, "mp", 2), late_got, *joint_corners))
        grad_act = partial[0] + got_0.astype(F32) + got.astype(F32)
        joint_sides = sides(joint_parts, *joint_corners)
        late_parts = add_rounded(late_parts[0::2], late_got)
    else:
        grad_act = collect_blocks(partial)
    g_qv = jnp.stack(
        [jnp.sum(grad_q, axis=0, dtype=F32), jnp.sum(grad_v, axis=0, dtype=F32)]
    ).reshape(2, 2, 1, columns)
    g_b_qv = lax.dynamic_update_slice(
        jnp.zeros((2, 2, group, columns), F32), g_qv, (0, 0, q, 0)
    ).reshape(2, width)
    grad_in, g_att_gain, g_att_shift = norm_backward(grad_act, att_unit, att_inv, att_gain)
    grad_resid = grad_resid + grad_in

    def joint_pieces(rows):
        rows = rows.reshape(-1, chan_q, width)
        parts = jnp.moveaxis(rows[: 4 * zs].reshape(4, zs, chan_q, width), 1, 0)
        parts = reordered(parts.reshape(zs, -1, width), m // 2)
        pair = rows[4 * zs :].reshape(3, 2, chan_q, width)
        pair = [
            lax.dynamic_index_in_dim(pair, which, 1, keepdims=False).reshape(-1, width)
            for which in (half, 1 - half)
        ]
        return parts, pair

    flight = {}

    def between(k, held):
        if k == 3:
            held = hold(held)
            flight["b"] = [swap(held[2], "mp", 1), swap(held[3], "mp", 1)]
            flight["late"] = swap(late_parts[1], "mp", 4)
        elif k == 2:
            *held, b_in, b_out = hold((*held, *flight["b"]))
            parts = add_parts(held[2], b_in, held[3], b_out, 4)
            flight["b_parts"] = [parts[r].reshape(-1, width) for r in range(4)]
            flight["corners"] = corners(flight["b_parts"])
        elif k == 1:
            *held, side_x, side_y, to_x, to_y, late_far = hold(
                (*held, *joint_sides, *flight["corners"], flight["late"])
            )
            flight["late"] = add_rounded(late_parts[0], late_far)
            b_sides = sides(flight["b_parts"], to_x, to_y)
            flight["mid"], flight["pair"] = joint_pieces(finish(joint_parts, side_x, side_y))
            mid_got = swap(flight["mid"][1::2], "mp", 2)
            a_got = [swap(held[2], "mp", 1), swap(held[3], "mp", 1)]
            flight["k1"] = (*a_got, *b_sides, mid_got)
        else:
            *held, a_in, a_out, b_x, b_y, mid_got = hold((*held, *flight["k1"]))
            parts = add_parts(held[2], a_in, held[3], a_out, 4)
            flight["a_parts"] = [parts[r].reshape(-1, width) for r in range(4)]
            flight["corners"] = corners(flight["a_parts"])
            b_sum = finish(flight["b_parts"], b_x, b_y).reshape(2, 2, hidden_q, width)
            flight["b_sum"] = b_sum[:, 0], swap(b_sum[:, 1], "mp", 2)
            mid = add_rounded(flight["mid"][0::2], mid_got)
            far = swap(jnp.concatenate([mid[1], flight["pair"][1]], axis=0), "mp", 4)
            flight["mid"] = jnp.concatenate([mid[0], flight["pair"][0]], axis=0), far
        return held

    grad_resid, mats_a, vecs_a = ffn_backward(
        grad_resid, saved_a, ffa_gain, blocks_a, between if rounds_fit() else None
    )
    g_embed = jnp.sum(grad_resid * flag_rows, axis=0, keepdims=True)
    back_first, back_second = send_back_parts(grad_resid.astype(BF))

    def hidden_order(parts):
        own, other = parts
        both = jnp.stack([jnp.where(core == 0, own, other), jnp.where(core == 0, other, own)])
        return both.reshape(2, zs, dp * hidden_q).transpose(1, 0, 2).reshape(-1, width)

    def relative_order(parts):
        rel = jnp.stack(parts).reshape(2, 2, dp, low, hidden_q)
        rel = rel.transpose(0, 3, 1, 2, 4).reshape(mp, dp, hidden_q)
        return rel[jnp.arange(mp) ^ m][:, jnp.arange(dp) ^ d].reshape(-1, width)

    small = (
        jnp.concatenate(
            [
                from_canon(jnp.concatenate([g_depth[:taps], g_conv_b_in[:2]], axis=0)),
                hidden_order(mats_b[1]),
                relative_order(mats_a[1]),
                g_b_qv,
                *vecs_b,
                g_final_gain,
                g_final_shift,
                g_conv_b_out,
                g_conv_gain,
                g_conv_shift,
                *vecs_a,
                g_embed,
                g_att_b_out,
                g_att_gain,
                g_att_shift,
            ],
            axis=0,
        )
    )
    if rounds_fit():
        b_own, b_near = flight["b_sum"]
        rest, far = flight["mid"]
        to_x, to_y, b_near, far, got = hold(
            (*flight["corners"], b_near, far, swap(small, "dp", 1))
        )
        small = small + got
        side_x, side_y = sides(flight["a_parts"], to_x, to_y)
        rest = jnp.concatenate([flight["late"], add_rounded(rest, far)], axis=0)
        side_x, side_y, b_far, got, rest, back_first, back_second = hold(
            (
                side_x,
                side_y,
                swap(add_rounded(b_own, b_near), "mp", 4),
                swap(small, "dp", 2),
                rest,
                back_first,
                back_second,
            )
        )
        small = small + got
        small = small + swap(small, "mp", 1)
        a_sum = finish(flight["a_parts"], side_x, side_y).reshape(2, 2, hidden_q, width)
        a_near, rest_x, rest_y, got = hold(
            (
                swap(a_sum[:, 1], "mp", 2),
                swap(rest, "dp", 1),
                swap(rest, "dp", 2),
                swap(small, "mp", 2),
            )
        )
        small = small + got
        small, back_first = hold((small + swap(small, "mp", 4), back_first))
        own = a_sum[:, 0].astype(F32) + a_near.astype(F32) + b_far.astype(F32)
        own = own.astype(BF).reshape(-1, width)
        cut = rest.shape[0] // 2
        by_x, by_y, rest_0, rest_1, back_first, back_second = hold(
            (
                swap(own, "dp", 1),
                swap(own, "dp", 2),
                swap(rest_y[:cut], "dp", 1),
                swap(rest_x[cut:], "dp", 2),
                send_straight(back_first),
                back_second,
            )
        )
        back_second = send_crossed(back_second)
        corner = [swap(by_y[:hidden_q], "dp", 1), swap(by_x[hidden_q:], "dp", 2)]
        first = jnp.stack([own, by_x, by_y, jnp.concatenate(corner, axis=0)])
        rest = jnp.stack([rest, rest_x, rest_y, jnp.concatenate([rest_0, rest_1], axis=0)])
        late_all = rest[:, : 2 * hidden_q]
        rest = rest[:, 2 * hidden_q :]
    else:
        joint = jnp.concatenate(joint, axis=0)
        joint = lax.psum_scatter(joint, "dp", scatter_dimension=1, tiled=True)
        mid_parts, pair = joint_pieces(joint)
        total = collect_plain(
            mats_a[0], mats_a[2], jnp.concatenate([late_parts, mid_parts], axis=1), pair
        )
        back_first, back_second = send_straight(back_first), send_crossed(back_second)
        first, late_all, rest = jnp.split(total, [2 * hidden_q, 4 * hidden_q], axis=1)
        small = combine_everywhere(small, jnp.add)
    if hidden_q % 128 == 0:
        g_ffa_in, g_ffa_out = unpack(first, d, hidden_q, 0)
        g_ffb_in, g_ffb_out = unpack(late_all, d, hidden_q, 0)
    else:
        pairs = []
        for part in (first, late_all):
            part = reordered(part, d).reshape(dp, 2, hidden_q, width).astype(F32)
            part = jnp.moveaxis(part, 1, 0).reshape(2, -1, width)
            pairs += [part[0].T, part[1]]
        g_ffa_in, g_ffa_out, g_ffb_in, g_ffb_out = pairs
    rest = reordered(rest, d).reshape(dp, 7, chan_q, width)
    rest = jnp.moveaxis(rest, 1, 0).reshape(7, columns, width).astype(F32)
    mid_total = rest[:4]
    g_att_qkv = rest[4:].transpose(0, 2, 1)

    total = small
    g_w_depth = own_columns(total[:taps])
    g_b_conv = own_columns(total[taps : taps + 2])
    at = taps + 2
    hidden_rows = mp * hidden_q * dp // width
    share = mats_b[1][0].shape[1] * 2 // mp

    def own_hidden(rows):
        return lax.dynamic_slice_in_dim(rows.reshape(-1), m * share, share, axis=0)

    g_ffb_b_in = own_hidden(total[at : at + hidden_rows])
    g_ffa_b_in = own_hidden(total[at + hidden_rows : at + 2 * hidden_rows])
    at = at + 2 * hidden_rows
    g_qv_out = own_columns(total[at : at + 2])
    e = total[at + 2 :]
    f = e[8:]

    def own_canon(vector):
        return own_columns(from_canon(vector))[0]

    mean_own = own_canon(batch_mean)
    var_own = own_canon(batch_var)
    g_scale = own_canon(sums[1:2] * inv_batch)
    g_shift = own_canon(sums[0:1])
    new_mean = 0.9 * running_mean + 0.1 * mean_own
    new_var = 0.9 * running_var + 0.1 * var_own * valid_count / (valid_count - 1.0)
    g_conv_w_in = jnp.stack([mid_total[0].T, mid_total[1].T])
    return (
        join_back(*layer_out),
        join_back(back_first, back_second),
        f[3],
        f[0],
        f[1],
        g_ffa_in,
        g_ffa_b_in,
        g_ffa_out,
        f[2],
        f[5],
        f[6],
        g_att_qkv,
        g_qv_out,
        mid_total[3],
        f[4],
        e[6],
        e[7],
        g_conv_w_in,
        g_b_conv,
        g_w_depth,
        g_scale,
        g_shift,
        mid_total[2],
        e[5],
        e[0],
        e[1],
        g_ffb_in,
        g_ffb_b_in,
        g_ffb_out,
        e[2],
        e[3],
        e[4],
        new_mean,
        new_var,
    )


def solution(mesh):
    return jax.shard_map(
        shards,
        mesh=mesh,
        in_specs=(
            P("dp", "mp", None),
            P("dp"),
            P("dp", "mp"),
            P(),
            P(),
            P(),
            P(None, "mp"),
            P("mp"),
            P("mp", None),
            P(),
            P(),
            P(),
            P(None, None, "mp"),
            P(None, "mp"),
            P("mp", None),
            P(),
            P(),
            P(),
            P(None, None, "mp"),
            P(None, "mp"),
            P(None, "mp"),
            P("mp"),
            P("mp"),
            P("mp"),
            P("mp"),
            P("mp", None),
            P(),
            P(),
            P(),
            P(None, "mp"),
            P("mp"),
            P("mp", None),
            P(),
            P(),
            P(),
            P("dp", "mp", None),
        ),
        out_specs=(
            P("dp", "mp", None),
            P("dp", "mp", None),
            P(),
            P(),
            P(),
            P(None, "mp"),
            P("mp"),
            P("mp", None),
            P(),
            P(),
            P(),
            P(None, None, "mp"),
            P(None, "mp"),
            P("mp", None),
            P(),
            P(),
            P(),
            P(None, None, "mp"),
            P(None, "mp"),
            P(None, "mp"),
            P("mp"),
            P("mp"),
            P("mp", None),
            P(),
            P(),
            P(),
            P(None, "mp"),
            P("mp"),
            P("mp", None),
            P(),
            P(),
            P(),
            P("mp"),
            P("mp"),
        ),
        check_vma=False,
    )
```

```python
import functools
import math

import jax
import jax.numpy as jnp
from jax import lax
from jax.experimental import pallas as pl
from jax.experimental.pallas import tpu as pltpu
from jax.sharding import PartitionSpec as P

HEAD = 64
EPS = 1e-05
BF = jnp.bfloat16
F32 = jnp.float32
LOG2E = math.log2(math.e)


def dot_nn(left, right):
    return lax.dot_general(left, right, (((1,), (0,)), ((), ())), preferred_element_type=F32)


def dot_nt(left, right):
    return lax.dot_general(left, right, (((1,), (1,)), ((), ())), preferred_element_type=F32)


def dot_tn(left, right):
    return lax.dot_general(left, right, (((0,), (0,)), ((), ())), preferred_element_type=F32)


def swap(values, axis, bit):
    count = lax.axis_size(axis)
    return lax.ppermute(values, axis, [(i, i ^ bit) for i in range(count)])


def bits_of(count):
    return [1 << k for k in range(count.bit_length() - 1)]


def norm_forward(values, gain_vec, shift_vec):
    row_mean = jnp.mean(values, axis=-1, keepdims=True)
    centred = values - row_mean
    inv_scale = lax.rsqrt(jnp.mean(centred * centred, axis=-1, keepdims=True) + EPS)
    unit_rows = centred * inv_scale
    return (unit_rows * gain_vec + shift_vec, unit_rows, inv_scale)


def norm_backward(grad_out, unit_rows, inv_scale, gain_vec):
    scaled = grad_out * gain_vec
    grad_in = inv_scale * (
        scaled
        - jnp.mean(scaled, axis=-1, keepdims=True)
        - unit_rows * jnp.mean(scaled * unit_rows, axis=-1, keepdims=True)
    )
    return (
        grad_in,
        jnp.sum(grad_out * unit_rows, axis=0, keepdims=True),
        jnp.sum(grad_out, axis=0, keepdims=True),
    )


def swish_slope(values):
    logistic = jax.nn.sigmoid(values)
    return logistic * (1.0 + values * (1.0 - logistic))


def split_halves(local):
    odd = lax.axis_index("mp") % 2
    first = lax.dynamic_index_in_dim(local, odd, 0, keepdims=False)
    second = lax.dynamic_index_in_dim(local, 1 - odd, 0, keepdims=False)
    return first, second


def send_halves(first, second):
    count = lax.axis_size("mp")
    group = count // 2
    straight = [(i, i // 2 + (group if i % 2 else 0)) for i in range(count)]
    crossed = [(i, i // 2 + (0 if i % 2 else group)) for i in range(count)]
    return lax.ppermute(first, "mp", straight), lax.ppermute(second, "mp", crossed)


def join_halves(got_a, got_b):
    low_half = lax.axis_index("mp") < lax.axis_size("mp") // 2
    lower = jnp.where(low_half, got_a, got_b)
    upper = jnp.where(low_half, got_b, got_a)
    return jnp.concatenate([lower, upper], axis=0)


def send_back_parts(rows):
    half = lax.axis_index("mp") // (lax.axis_size("mp") // 2)
    frames = rows.shape[0] // 2
    lower, upper = rows[:frames], rows[frames:]
    return jnp.where(half == 0, lower, upper), jnp.where(half == 0, upper, lower)


def send_straight(rows):
    count = lax.axis_size("mp")
    group = count // 2
    return lax.ppermute(
        rows, "mp", [(i // 2 + (group if i % 2 else 0), i) for i in range(count)]
    )


def send_crossed(rows):
    count = lax.axis_size("mp")
    group = count // 2
    return lax.ppermute(
        rows, "mp", [(i // 2 + (0 if i % 2 else group), i) for i in range(count)]
    )


def send_back(rows):
    first, second = send_back_parts(rows)
    return send_straight(first), send_crossed(second)


def join_back(got_a, got_b):
    even = lax.axis_index("mp") % 2 == 0
    return jnp.stack([jnp.where(even, got_a, got_b), jnp.where(even, got_b, got_a)]).astype(F32)


hold = lax.optimization_barrier


def rounds_fit():
    return lax.axis_size("dp") == 4 and lax.axis_size("mp") == 8


def add_rounded(one, two):
    return (one.astype(F32) + two.astype(F32)).astype(BF)


def reordered(parts, index):
    count = parts.shape[0]
    return jnp.concatenate(
        [lax.dynamic_slice_in_dim(parts, k ^ index, 1, axis=0) for k in range(count)], axis=0
    )


def joined_z(parts):
    stacked = jnp.stack([parts[r] for r in sorted(parts)])
    ordered = jnp.moveaxis(reordered(stacked, lax.axis_index("mp") // 2), 0, 1)
    return ordered.reshape(-1, *ordered.shape[2:])


def spread_z(piece):
    parts = {0: piece}
    for bit in reversed(bits_of(lax.axis_size("mp"))[1:]):
        for index in list(parts):
            parts[index | bit] = swap(parts[index], "mp", bit)
    return parts


def spread_dp(pair):
    count = lax.axis_size("dp")
    if count != 4:
        for bit in bits_of(count):
            pair = jnp.concatenate([pair, swap(pair, "dp", bit)], axis=1)
        return pair
    by_x, by_y = hold((swap(pair, "dp", 1), swap(pair, "dp", 2)))
    both = jnp.stack([swap(by_y[0], "dp", 1), swap(by_x[1], "dp", 2)])
    return jnp.concatenate([pair, by_x, by_y, both], axis=1)


def spread_small(small):
    for bit in bits_of(lax.axis_size("mp")):
        small = jnp.concatenate([small, swap(small, "mp", bit)], axis=0)
    return small


def spread_rounds(piece, small, middle, late, halves, far_weight, counts):
    far_bit = lax.axis_size("mp") // 2
    if not rounds_fit():
        parts = spread_z(piece)
        near, far = (
            spread_dp(
                jnp.concatenate([parts[r] for r in sorted(parts) if (r & far_bit) == want], axis=1)
            )
            for want in (0, far_bit)
        )
        blocks = (near, swap(near, "mp", 1), far, swap(far, "mp", 1))
        return (
            blocks,
            spread_small(small[None]),
            joined_z(spread_z(middle)),
            joined_z(spread_z(late)),
            send_halves(*halves),
            swap(far_weight, "mp", far_bit),
            counts,
        )
    small = jnp.stack([small, swap(small, "mp", 1)])
    near, far, halves, got, counts, middle, late = hold(
        (
            swap(piece, "mp", 2),
            swap(piece, "mp", 4),
            halves,
            swap(small, "mp", 2),
            counts,
            middle,
            late,
        )
    )
    small = jnp.concatenate([small, got], axis=0)
    part_a = jnp.concatenate([piece, near], axis=1)
    a_x, a_y, far_near, far_weight, small, halves = hold(
        (
            swap(part_a, "dp", 1),
            swap(part_a, "dp", 2),
            swap(far, "mp", 2),
            far_weight,
            small,
            send_halves(*halves),
        )
    )
    part_b = jnp.concatenate([far, far_near], axis=1)
    ahead = jnp.concatenate([middle.reshape(2, -1, middle.shape[-1]), late], axis=1)
    b_x, b_y, a_0, a_1, far_weight, ahead = hold(
        (
            swap(part_b, "dp", 1),
            swap(part_b, "dp", 2),
            swap(a_y[0], "dp", 1),
            swap(a_x[1], "dp", 2),
            swap(far_weight, "mp", 4),
            ahead,
        )
    )
    all_a = jnp.concatenate([part_a, a_x, a_y, jnp.stack([a_0, a_1])], axis=1)
    b_0, b_1, other_a, ahead_near, mid_far, got = hold(
        (
            swap(b_y[0], "dp", 1),
            swap(b_x[1], "dp", 2),
            swap(all_a, "mp", 1),
            swap(ahead, "mp", 2),
            swap(middle, "mp", 4),
            swap(small, "mp", 4),
        )
    )
    small = jnp.concatenate([small, got], axis=0)
    cut = ahead.shape[1] - late.shape[1]
    all_b = jnp.concatenate([part_b, b_x, b_y, jnp.stack([b_0, b_1])], axis=1)
    return (
        (all_a, other_a, all_b, swap(all_b, "mp", 1)),
        small,
        {0: middle, 2: ahead_near[:, :cut].reshape(middle.shape), 4: mid_far},
        {0: late, 2: ahead_near[:, cut:]},
        halves,
        far_weight,
        counts,
    )


def z_groups():
    count = lax.axis_size("mp")
    return [list(range(core, count, 2)) for core in range(2)]


def collect_z_relative(parts):
    live = {2 * k: parts[k] for k in range(parts.shape[0])}
    for bit in bits_of(lax.axis_size("mp"))[1:]:
        for index in [r for r in live if r & bit]:
            live[index ^ bit] = add_rounded(live[index ^ bit], swap(live.pop(index), "mp", bit))
    return live[0]


def halve_z(parts, bit):
    return add_rounded(parts[0::2], swap(parts[1::2], "mp", bit))


def collect_dp(pair):
    for bit in reversed(bits_of(lax.axis_size("dp"))):
        rows = pair.shape[1] // 2
        pair = add_rounded(pair[:, :rows], swap(pair[:, rows:], "dp", bit))
    return pair


def corners(parts):
    half = parts[3].shape[0] // 2
    return swap(parts[3][:half], "dp", 1), swap(parts[3][half:], "dp", 2)


def sides(parts, to_x, to_y):
    half = parts[0].shape[0] // 2
    via_x = jnp.concatenate([parts[1][:half], add_rounded(parts[1][half:], to_y)], axis=0)
    via_y = jnp.concatenate([add_rounded(parts[2][:half], to_x), parts[2][half:]], axis=0)
    return swap(via_x, "dp", 1), swap(via_y, "dp", 2)


def finish(parts, got_x, got_y):
    return (parts[0].astype(F32) + got_x.astype(F32) + got_y.astype(F32)).astype(BF)


def collect_plain(grads_in, grads_out, z_parts, far_part):
    far_bit = lax.axis_size("mp") // 2
    sums = []
    for far in (0, 1):
        own, other = (jnp.stack([grads_in[2 * far + k], grads_out[2 * far + k]]) for k in range(2))
        sums.append(collect_dp(add_rounded(own, swap(other, "mp", 1))))
    count = lax.axis_size("mp") // 4
    stacked = jnp.concatenate([jnp.stack(jnp.split(part, count, axis=1)) for part in sums], axis=0)
    own = collect_z_relative(stacked)
    own = jnp.concatenate(
        [
            own.reshape(-1, own.shape[-1]),
            collect_z_relative(z_parts),
            add_rounded(far_part[0], swap(far_part[1], "mp", far_bit)),
        ],
        axis=0,
    )
    for bit in bits_of(lax.axis_size("dp")):
        own = jnp.concatenate([own, swap(own, "dp", bit)], axis=0)
    return own.reshape(lax.axis_size("dp"), -1, own.shape[-1])


def combine_everywhere(rows, combine, beside=None):
    order = [("mp", bit) for bit in bits_of(lax.axis_size("mp"))]
    order[1:1] = [("dp", bit) for bit in bits_of(lax.axis_size("dp"))]
    for step, (axis, bit) in enumerate(order):
        got = swap(rows, axis, bit)
        if beside is not None and step < len(beside) and beside[step] is not None:
            got, beside[step] = hold((got, beside[step]))
        rows = combine(rows, got)
    return rows


def ffn_forward(resid, gain_vec, shift_vec, blocks, b_out, beside=None):
    normed, unit_rows, inv_scale = norm_forward(resid, gain_vec, shift_vec)
    act = normed.astype(BF)
    branch = b_out
    uppers, hiddens = [], []
    for w_in_t, w_out, b_in in blocks:
        upper = dot_nt(act, w_in_t) + b_in
        hidden = jax.nn.silu(upper).astype(BF)
        branch = branch + dot_nn(hidden, w_out)
        uppers.append(upper)
        hiddens.append(hidden)
        if beside is not None and 2 * len(uppers) == len(blocks):
            branch, beside[0] = hold((branch, beside[0]))
    return branch, (unit_rows, inv_scale, act, uppers, hiddens)


def ffn_backward(grad_resid, saved, gain_vec, blocks, between=None):
    unit_rows, inv_scale, act, uppers, hiddens = saved
    grad_branch = (0.5 * grad_resid).astype(BF)
    grad_b_out = jnp.sum(grad_branch, axis=0, dtype=F32, keepdims=True)
    grad_act = 0.0
    count = len(blocks)
    later = []
    grads_in, grads_out, grads_b = [None] * count, [None] * count, [None] * count
    for k in reversed(range(count)):
        w_in_t, w_out, _ = blocks[k]
        grad_hidden = dot_nt(grad_branch, w_out)
        grad_upper = (grad_hidden * swish_slope(uppers[k])).astype(BF)
        if between is not None:
            grad_upper = between(("upper", k), grad_upper)
        grads_b[k] = jnp.sum(grad_upper, axis=0, dtype=F32, keepdims=True)
        grads_in[k] = dot_tn(grad_upper, act).astype(BF)
        grads_out[k] = dot_tn(hiddens[k], grad_branch).astype(BF)
        if between is not None and k < 2:
            grad_branch, grads_in[k], grads_out[k] = between(
                ("block", k), (grad_branch, grads_in[k], grads_out[k])
            )
            later.append(grad_upper)
            continue
        grad_act = grad_act + dot_nn(grad_upper, w_in_t)
        if between is not None:
            grad_branch, grads_in[k], grads_out[k], grad_act = between(
                ("block", k), (grad_branch, grads_in[k], grads_out[k], grad_act)
            )
    if later:
        later = between(("rest", None), later)
        for k, grad_upper in zip((1, 0), later, strict=True):
            grad_act = grad_act + dot_nn(grad_upper, blocks[k][0])
    grad_in, grad_gain, grad_shift = norm_backward(grad_act, unit_rows, inv_scale, gain_vec)
    return (
        grad_resid + grad_in,
        (grads_in, grads_b, grads_out),
        (grad_gain, grad_shift, grad_b_out),
    )


def pair_mask(shape, head):
    lane = lax.broadcasted_iota(jnp.int32, shape, len(shape) - 1)
    return (lane // HEAD) == head


def attend_kernel(q_ref, k_ref, v_ref, bias_ref, out_ref, wide_ref, lse_ref):
    query, key, value = q_ref[...], k_ref[...], v_ref[...]
    bias = bias_ref[...]
    factor = LOG2E / math.sqrt(HEAD)
    mixed, logs = [], []
    for head in range(2):
        masked = jnp.where(pair_mask(query.shape, head), query, jnp.zeros_like(query))
        scores = dot_nt(masked, key) * factor + bias
        row_max = jnp.max(scores, axis=-1, keepdims=True)
        shifted = jnp.exp2(scores - row_max)
        total = jnp.sum(shifted, axis=-1, keepdims=True)
        mixed.append(dot_nn(shifted.astype(BF), value) * (1.0 / total))
        logs.append(row_max + jnp.log2(total))
    first = pair_mask(mixed[0].shape, 0)
    wide = jnp.where(first, mixed[0], mixed[1])
    wide_ref[...] = wide
    out_ref[...] = wide.astype(BF)
    lse_ref[...] = jnp.where(first, logs[0], logs[1])


def attend_forward(query, key, value, bias, block):
    frames, columns = query.shape
    pairs = columns // (2 * HEAD)
    rows_spec = pl.BlockSpec((block, 2 * HEAD), lambda p, i: (i, p))
    whole_spec = pl.BlockSpec((frames, 2 * HEAD), lambda p, i: (0, p))
    return pl.pallas_call(
        attend_kernel,
        grid=(pairs, frames // block),
        in_specs=[rows_spec, whole_spec, whole_spec, pl.BlockSpec((1, frames), lambda p, i: (0, 0))],
        out_specs=[rows_spec, rows_spec, rows_spec],
        out_shape=[
            jax.ShapeDtypeStruct((frames, columns), BF),
            jax.ShapeDtypeStruct((frames, columns), F32),
            jax.ShapeDtypeStruct((frames, columns), F32),
        ],
        compiler_params=pltpu.CompilerParams(vmem_limit_bytes=56 * 1024 * 1024),
        cost_estimate=pl.CostEstimate(
            flops=8 * frames * frames * columns,
            bytes_accessed=12 * frames * columns,
            transcendentals=frames * frames * columns // HEAD,
        ),
        name="attend_forward",
    )(query, key, value, bias)


def attend_back_kernel(
    q_ref, k_ref, v_ref, g_ref, wide_ref, lse_ref, bias_ref, dq_ref, dk_ref, dv_ref, dk_acc, dv_acc
):
    step = pl.program_id(1)
    query, key, value, grad = q_ref[...], k_ref[...], v_ref[...], g_ref[...]
    bias = bias_ref[...]
    lse = lse_ref[...]
    factor = LOG2E / math.sqrt(HEAD)
    scale = 1.0 / math.sqrt(HEAD)
    both = grad.astype(F32) * wide_ref[...]
    dq, new_dk, new_dv = [], 0.0, 0.0
    for head in range(2):
        mask = pair_mask(query.shape, head)
        query_h = jnp.where(mask, query, jnp.zeros_like(query))
        grad_h = jnp.where(mask, grad, jnp.zeros_like(grad))
        scores = dot_nt(query_h, key) * factor + bias
        probs = jnp.exp2(scores - lse[:, head * HEAD : head * HEAD + 1])
        grad_probs = dot_nt(grad_h, value)
        row_dot = jnp.sum(jnp.where(mask, both, 0.0), axis=-1, keepdims=True)
        grad_scores = (probs * (grad_probs - row_dot)).astype(BF)
        new_dv = new_dv + dot_tn(grad_h, probs.astype(BF))
        dq.append(dot_nn(grad_scores, key))
        new_dk = new_dk + dot_tn(query_h, grad_scores)
    first = pair_mask(dq[0].shape, 0)
    dq_ref[...] = (jnp.where(first, dq[0], dq[1]) * scale).astype(BF)

    @pl.when(step == 0)
    def _():
        dk_acc[...] = new_dk
        dv_acc[...] = new_dv

    @pl.when(step > 0)
    def _():
        dk_acc[...] += new_dk
        dv_acc[...] += new_dv

    @pl.when(step == pl.num_programs(1) - 1)
    def _():
        dk_ref[...] = (dk_acc[...] * scale).T.astype(BF)
        dv_ref[...] = dv_acc[...].T.astype(BF)


def attend_backward(query, key, value, grad, wide, lse, bias, block):
    frames, columns = query.shape
    pairs = columns // (2 * HEAD)
    rows_spec = pl.BlockSpec((block, 2 * HEAD), lambda p, i: (i, p))
    whole_spec = pl.BlockSpec((frames, 2 * HEAD), lambda p, i: (0, p))
    shape = jax.ShapeDtypeStruct((frames, columns), BF)
    return pl.pallas_call(
        attend_back_kernel,
        grid=(pairs, frames // block),
        in_specs=[
            rows_spec,
            whole_spec,
            whole_spec,
            rows_spec,
            rows_spec,
            rows_spec,
            pl.BlockSpec((1, frames), lambda p, i: (0, 0)),
        ],
        out_specs=[rows_spec, whole_spec, whole_spec],
        out_shape=[shape, shape, shape],
        scratch_shapes=[
            pltpu.VMEM((2 * HEAD, frames), F32),
            pltpu.VMEM((2 * HEAD, frames), F32),
        ],
        compiler_params=pltpu.CompilerParams(vmem_limit_bytes=56 * 1024 * 1024),
        cost_estimate=pl.CostEstimate(
            flops=20 * frames * frames * columns,
            bytes_accessed=20 * frames * columns,
            transcendentals=frames * frames * columns // HEAD,
        ),
        name="attend_backward",
    )(query, key, value, grad, wide, lse, bias)


def add_parts_kernel(one_ref, got_one_ref, two_ref, got_two_ref, out_ref):
    out_ref[0] = (one_ref[...].astype(F32) + got_one_ref[...].astype(F32)).astype(BF)
    out_ref[1] = (two_ref[...].astype(F32) + got_two_ref[...].astype(F32)).astype(BF)


def add_parts(one, got_one, two, got_two, parts):
    rows, width = one.shape
    part = rows // parts
    step = math.gcd(part, 256)
    steps = part // step
    spec = pl.BlockSpec((step, width), lambda p, j: (p * steps + j, 0))
    return pl.pallas_call(
        add_parts_kernel,
        grid=(parts, steps),
        in_specs=[spec] * 4,
        out_specs=pl.BlockSpec((None, 2, step, width), lambda p, j: (p, 0, j, 0)),
        out_shape=jax.ShapeDtypeStruct((parts, 2, part, width), BF),
        compiler_params=pltpu.CompilerParams(vmem_limit_bytes=32 * 1024 * 1024),
        cost_estimate=pl.CostEstimate(
            flops=2 * rows * width, bytes_accessed=12 * rows * width, transcendentals=0
        ),
        name="add_parts",
    )(one, got_one, two, got_two)


def unpack_kernel(index_ref, *refs, rows):
    parts, in_ref, out_ref = refs[:-2], refs[-2], refs[-1]
    for r, part_ref in enumerate(parts):
        start = pl.multiple_of((index_ref[0] ^ r) * rows, rows)
        in_ref[:, pl.ds(start, rows)] = part_ref[:rows].astype(F32).T
        out_ref[pl.ds(start, rows)] = part_ref[rows : 2 * rows].astype(F32)


def unpack(parts, index, rows):
    count = len(parts)
    width = parts[0].shape[1]
    spec = pl.BlockSpec((2 * rows, width), lambda i, at: (0, 0))
    return pl.pallas_call(
        functools.partial(unpack_kernel, rows=rows),
        grid_spec=pltpu.PrefetchScalarGridSpec(
            num_scalar_prefetch=1,
            grid=(1,),
            in_specs=[spec] * count,
            out_specs=[
                pl.BlockSpec((width, count * rows), lambda i, at: (0, 0)),
                pl.BlockSpec((count * rows, width), lambda i, at: (0, 0)),
            ],
        ),
        out_shape=[
            jax.ShapeDtypeStruct((width, count * rows), F32),
            jax.ShapeDtypeStruct((count * rows, width), F32),
        ],
        compiler_params=pltpu.CompilerParams(vmem_limit_bytes=32 * 1024 * 1024),
        cost_estimate=pl.CostEstimate(
            flops=0, bytes_accessed=12 * count * rows * width, transcendentals=0
        ),
        name="unpack",
    )(index.reshape(1), *parts)


def lay_out(buffer, before, rows, after, halo):
    count = rows.shape[0]
    buffer[:halo] = before[...]
    buffer[halo : halo + count] = rows[...]
    buffer[halo + count :] = after[...]


def depth_kernel(
    before_ref, rows_ref, after_ref, taps_ref, visible_ref, depth_ref, stats_ref, padded, *, taps
):
    count, lanes = depth_ref.shape
    halo = before_ref.shape[0]
    first = halo - taps // 2
    lay_out(padded, before_ref, rows_ref, after_ref, halo)
    depth = jnp.zeros((count, lanes), F32)
    for phase in range(8):
        more = (taps - 1 - phase) // 8
        base = padded[first + phase : first + phase + count + 8 * more]
        for step in range(more + 1):
            tap = 8 * step + phase
            depth = depth + base[8 * step : 8 * step + count] * taps_ref[tap : tap + 1]
    depth_ref[...] = depth
    visible = visible_ref[...]
    frames = jnp.sum(visible, axis=0, keepdims=True)
    mean = jnp.sum(depth * visible, axis=0, keepdims=True) / jnp.maximum(frames, 1.0)
    apart = (depth - mean) * visible
    stats_ref[0:1] = jnp.broadcast_to(frames, (1, lanes))
    stats_ref[1:2] = mean
    stats_ref[2:3] = jnp.sum(apart * apart, axis=0, keepdims=True)
    stats_ref[3:] = jnp.zeros((5, lanes), F32)


def depth_forward(rows, around, taps_rows, visible, taps):
    count, width = rows.shape
    lanes = 128
    halo = around[0].shape[0]

    def column(height):
        return pl.BlockSpec((height, lanes), lambda j: (0, j))

    return pl.pallas_call(
        functools.partial(depth_kernel, taps=taps),
        grid=(width // lanes,),
        in_specs=[
            column(halo),
            column(count),
            column(halo),
            column(taps_rows.shape[0]),
            pl.BlockSpec((count, 1), lambda j: (0, 0)),
        ],
        out_specs=[column(count), column(8)],
        out_shape=[
            jax.ShapeDtypeStruct((count, width), F32),
            jax.ShapeDtypeStruct((8, width), F32),
        ],
        scratch_shapes=[pltpu.VMEM((count + 2 * halo, lanes), F32)],
        cost_estimate=pl.CostEstimate(
            flops=2 * taps * count * width, bytes_accessed=9 * count * width, transcendentals=0
        ),
        name="depth_forward",
    )(around[0], rows, around[1], taps_rows, visible)


def depth_back_kernel(
    gbefore_ref,
    grad_ref,
    gafter_ref,
    before_ref,
    rows_ref,
    after_ref,
    taps_ref,
    visible_ref,
    value_ref,
    logistic_ref,
    gvalue_ref,
    ggate_ref,
    gtaps_ref,
    gbias_ref,
    gpadded,
    padded,
    *,
    taps,
):
    count, lanes = grad_ref.shape
    halo = before_ref.shape[0]
    first = halo - taps // 2
    lay_out(gpadded, gbefore_ref, grad_ref, gafter_ref, halo)
    lay_out(padded, before_ref, rows_ref, after_ref, halo)
    tap_rows = taps_ref[...]
    sums = [jnp.zeros((8, lanes), F32) for _ in range(taps)]
    tile = math.gcd(count, 32)
    gvalue, ggate = 0.0, 0.0
    for start in range(0, count, tile):
        here = slice(start, start + tile)
        grad = grad_ref[here]
        total = jnp.zeros((tile, lanes), F32)
        for tap in range(taps):
            there = slice(first + start + tap, first + start + tap + tile)
            total = total + gpadded[there] * tap_rows[taps - 1 - tap : taps - tap]
            product = (grad * padded[there]).reshape(tile // 8, 8, lanes)
            sums[tap] = sums[tap] + jnp.sum(product, axis=0)
        grad_gated = total * visible_ref[here]
        logistic = logistic_ref[here]
        value_part = (grad_gated * logistic).astype(BF)
        gate_part = (grad_gated * value_ref[here] * logistic * (1.0 - logistic)).astype(BF)
        gvalue_ref[here] = value_part
        ggate_ref[here] = gate_part
        gvalue = gvalue + jnp.sum(value_part.astype(F32), axis=0, keepdims=True)
        ggate = ggate + jnp.sum(gate_part.astype(F32), axis=0, keepdims=True)
    for tap in range(taps):
        gtaps_ref[tap : tap + 1] = jnp.sum(sums[tap], axis=0, keepdims=True)
    gbias_ref[0:1] = gvalue
    gbias_ref[1:2] = ggate
    gbias_ref[2:] = jnp.zeros((6, lanes), F32)


def depth_backward(grad, garound, rows, around, taps_rows, visible, value, logistic, taps):
    count, width = rows.shape
    lanes = 128
    halo = around[0].shape[0]

    def column(height):
        return pl.BlockSpec((height, lanes), lambda j: (0, j))

    return pl.pallas_call(
        functools.partial(depth_back_kernel, taps=taps),
        grid=(width // lanes,),
        in_specs=[
            column(halo),
            column(count),
            column(halo),
            column(halo),
            column(count),
            column(halo),
            column(taps_rows.shape[0]),
            pl.BlockSpec((count, 1), lambda j: (0, 0)),
            column(count),
            column(count),
        ],
        out_specs=[column(count), column(count), column(taps_rows.shape[0]), column(8)],
        out_shape=[
            jax.ShapeDtypeStruct((count, width), BF),
            jax.ShapeDtypeStruct((count, width), BF),
            jax.ShapeDtypeStruct(taps_rows.shape, F32),
            jax.ShapeDtypeStruct((8, width), F32),
        ],
        scratch_shapes=[pltpu.VMEM((count + 2 * halo, lanes), F32)] * 2,
        cost_estimate=pl.CostEstimate(
            flops=4 * taps * count * width, bytes_accessed=24 * count * width, transcendentals=0
        ),
        name="depth_backward",
    )(
        garound[0], grad, garound[1], around[0], rows, around[1], taps_rows, visible, value, logistic
    )


def spread_blocks(local, group):
    blocks = {0: local}
    for bit in reversed(bits_of(group)):
        for index in list(blocks):
            blocks[index | bit] = swap(blocks[index], "mp", bit)
    return [blocks[r] for r in range(group)]


def collect_blocks(parts):
    live = dict(enumerate(parts))
    for bit in bits_of(len(parts)):
        for index in [r for r in live if not r & bit]:
            sent = swap(live.pop(index | bit).astype(BF), "mp", bit)
            live[index] = live[index] + sent.astype(F32)
    return live[0]


def exchange_blocks(parts):
    return [parts[0]] + [swap(parts[r], "mp", r) for r in range(1, len(parts))]


def shards(
    frames,
    lengths,
    mask_flags,
    mask_embed,
    ffa_gain,
    ffa_shift,
    ffa_w_in,
    ffa_b_in,
    ffa_w_out,
    ffa_b_out,
    att_gain,
    att_shift,
    att_w_qkv,
    att_b_qv,
    att_w_out,
    att_b_out,
    conv_gain,
    conv_shift,
    conv_w_in,
    conv_b_in,
    conv_w_depth,
    batch_scale,
    batch_shift,
    running_mean,
    running_var,
    conv_w_out,
    conv_b_out,
    ffb_gain,
    ffb_shift,
    ffb_w_in,
    ffb_b_in,
    ffb_w_out,
    ffb_b_out,
    final_gain,
    final_shift,
    cotangent,
):
    mask_embed = mask_embed[None]
    ffa_gain = ffa_gain[None]
    ffa_shift = ffa_shift[None]
    ffa_b_out = ffa_b_out[None]
    att_gain = att_gain[None]
    att_shift = att_shift[None]
    att_b_out = att_b_out[None]
    conv_gain = conv_gain[None]
    conv_shift = conv_shift[None]
    conv_b_out = conv_b_out[None]
    ffb_gain = ffb_gain[None]
    ffb_shift = ffb_shift[None]
    ffb_b_out = ffb_b_out[None]
    final_gain = final_gain[None]
    final_shift = final_shift[None]
    dp = lax.axis_size("dp")
    mp = lax.axis_size("mp")
    zs = mp // 2
    group = mp // 2
    d = lax.axis_index("dp")
    m = lax.axis_index("mp")
    core = m % 2
    half = m // group
    q = m % group
    width = frames.shape[2]
    columns = width // mp
    rows_local = 2 * mask_flags.shape[1]
    hidden_q = ffa_b_in.shape[0] // dp
    chan_q = columns // dp
    taps = conv_w_depth.shape[0]
    reach = taps // 2

    small = jnp.concatenate(
        [
            ffa_b_in.astype(F32).reshape(-1, columns),
            ffb_b_in.astype(F32).reshape(-1, columns),
            conv_b_in,
            conv_w_depth,
            batch_scale[None],
            batch_shift[None],
            att_b_qv,
        ],
        axis=0,
    )
    low = mp // 4

    def relative_bias(far, near_core):
        first = far * (mp // 2) + near_core
        part = bias_rel[first : first + 2 * low : 2]
        return part.transpose(1, 0, 2).reshape(1, -1)


    def hidden_bias(rows):
        both = rows.reshape(zs, 2, dp * hidden_q).transpose(1, 0, 2).reshape(2, -1)
        own = lax.dynamic_slice_in_dim(both, core, 1, axis=0)
        other = lax.dynamic_slice_in_dim(both, 1 - core, 1, axis=0)
        return own, other

    def to_canon(rows):
        lead = rows.shape[:-1]
        split = rows.reshape(*lead, zs, 2, columns)
        return jnp.moveaxis(split, -3, -2).reshape(*lead, width)

    def from_canon(rows):
        lead = rows.shape[:-1]
        split = rows.reshape(*lead, 2, zs, columns)
        return jnp.moveaxis(split, -3, -2).reshape(*lead, width)

    def own_columns(rows):
        return lax.dynamic_slice_in_dim(rows, m * columns, columns, axis=-1)

    def hidden_pieces(w_in, w_out):
        piece_in = lax.dynamic_slice_in_dim(w_in, d * hidden_q, hidden_q, axis=1).T
        piece_out = lax.dynamic_slice_in_dim(w_out, d * hidden_q, hidden_q, axis=0)
        return piece_in, piece_out

    def channel_piece(rows):
        return lax.dynamic_slice_in_dim(rows, d * chan_q, chan_q, axis=0)

    kinds = [conv_w_in[0].T, conv_w_in[1].T, conv_w_out, att_w_out]
    valid_count = jnp.sum(lengths).astype(F32)
    for bit in bits_of(dp):
        valid_count = valid_count + swap(valid_count, "dp", bit)
    flags = jnp.pad(mask_flags.astype(BF), ((0, 0), (0, 16 * width - mask_flags.shape[1])))
    frames = jnp.concatenate([frames, flags.reshape(2, 16, width)], axis=1)
    per = ffa_b_in.shape[0] // columns
    gathered, small, mid_z, late_z, halves, w_other, valid_count = spread_rounds(
        jnp.stack(hidden_pieces(ffa_w_in, ffa_w_out)),
        jnp.pad(small, ((0, -small.shape[0] % 16), (0, 0))).reshape(-1, width),
        jnp.stack([channel_piece(rows) for rows in kinds]),
        jnp.stack(hidden_pieces(ffb_w_in, ffb_w_out)),
        split_halves(frames),
        att_w_qkv,
        valid_count,
    )
    small = small.reshape(mp, -1, columns)[:, : 2 * per + 6 + taps]
    bias_rel = small[:, :per].reshape(mp, dp, hidden_q)[:, jnp.arange(dp) ^ d]
    small = small[jnp.arange(mp) ^ m]
    bias_b = hidden_bias(small[:, per : 2 * per])
    small = small[:, 2 * per :]
    conv_small = to_canon(jnp.moveaxis(small[:, : 4 + taps], 0, 1).reshape(-1, width))
    b_qv = jnp.moveaxis(small[:, 4 + taps :], 0, 1).reshape(2, 2, group, columns)
    b_qv = lax.dynamic_index_in_dim(b_qv, q, 2, keepdims=False).reshape(2, -1)
    frames_local = mask_flags.shape[1]
    rows_in = join_halves(*(part[:frames_local] for part in halves))
    flag_rows = [part[frames_local:].reshape(-1)[:frames_local, None] for part in halves]
    flag_rows = join_halves(*flag_rows).astype(F32)
    c_b_in = [conv_small[0:1], conv_small[1:2]]
    c_depth = jnp.pad(conv_small[2 : 2 + taps], ((0, -taps % 8), (0, 0)))
    c_scale = conv_small[2 + taps : 3 + taps]
    c_shift = conv_small[3 + taps : 4 + taps]
    blocks_a = [
        (gathered[k][0], gathered[k][1], relative_bias(k // 2, k % 2)) for k in range(4)
    ]
    if not rounds_fit():
        mid_own = lax.all_gather(mid_z, "dp", axis=1, tiled=True)
        late_own = lax.all_gather(late_z, "dp", axis=1, tiled=True)

    length = lax.dynamic_index_in_dim(lengths, half, 0, keepdims=False)
    place = q * rows_local + jnp.arange(rows_local)
    visible = (place < length).astype(F32)[:, None]
    key_place = ((jnp.arange(group) ^ q)[:, None] * rows_local + jnp.arange(rows_local)).reshape(1, -1)
    key_bias = jnp.where(key_place < length, 0.0, -1e30).astype(F32)

    resid_a = rows_in.astype(F32) + flag_rows * mask_embed
    if rounds_fit():
        beside = [swap(mid_z[4], "mp", 2)]
        branch, saved_a = ffn_forward(resid_a, ffa_gain, ffa_shift, blocks_a, ffa_b_out, beside)
        mid_z = joined_z({**mid_z, 6: beside[0]})
        mid_own = lax.all_gather(mid_z, "dp", axis=1, tiled=True)
    else:
        branch, saved_a = ffn_forward(resid_a, ffa_gain, ffa_shift, blocks_a, ffa_b_out)
    resid_b = resid_a + 0.5 * branch

    normed, att_unit, att_inv = norm_forward(resid_b, att_gain, att_shift)
    att_act = normed.astype(BF)
    if rounds_fit():
        near, by_core_act, late_far = hold(
            (swap(att_act, "mp", 2), swap(att_act, "mp", 1), swap(late_z[0], "mp", 4))
        )
        blocks = [att_act, by_core_act, near, swap(near, "mp", 1)]
    else:
        blocks = spread_blocks(att_act, group)
    w_qkv = jnp.concatenate(
        [jnp.where(half == 0, att_w_qkv, w_other), jnp.where(half == 0, w_other, att_w_qkv)], axis=2
    )
    att_rows = jnp.concatenate(blocks, axis=0)
    query = (dot_nn(att_rows, w_qkv[0]) + b_qv[0]).astype(BF)
    key = dot_nn(att_rows, w_qkv[1]).astype(BF)
    value = (dot_nn(att_rows, w_qkv[2]) + b_qv[1]).astype(BF)
    if rounds_fit():
        query, key, value, late_both, mid_own = hold(
            (query, key, value, swap(late_far, "mp", 2), mid_own)
        )
        late_z = joined_z({**late_z, 4: late_far, 6: late_both})
        late_own = lax.all_gather(late_z, "dp", axis=1, tiled=True)
    block = group * rows_local // 2
    mixed_cols, mixed_wide, lse = attend_forward(query, key, value, key_bias, block)
    mid_other = swap(mid_own, "mp", 1)
    parts = [mixed_cols[r * rows_local : (r + 1) * rows_local] for r in range(group)]
    parts = exchange_blocks(parts)
    mid = jnp.stack(
        [
            jnp.where(core == 0, one, two).reshape(4, zs, columns, width)
            for one, two in ((mid_own, mid_other), (mid_other, mid_own))
        ],
        axis=1,
    )
    conv_value_w, conv_gate_w, conv_out_w = (mid[k].reshape(width, width) for k in range(3))
    att_out_w = mid[3].transpose(1, 0, 2, 3).reshape(2, group, columns, width)
    att_out_w = reordered(jnp.moveaxis(att_out_w, 1, 0), q).reshape(width, width)
    *parts, conv_value_w, conv_gate_w, conv_out_w, att_out_w, cotangent = hold(
        (*parts, conv_value_w, conv_gate_w, conv_out_w, att_out_w, cotangent)
    )
    cot_halves = send_halves(*split_halves(cotangent))
    mixed = jnp.concatenate(parts, axis=1)
    resid_c = resid_b + (dot_nn(mixed, att_out_w) + att_b_out)

    normed, conv_unit, conv_inv = norm_forward(resid_c, conv_gain, conv_shift)
    conv_act = normed.astype(BF)
    pre_value = dot_nt(conv_act, conv_value_w) + c_b_in[0]
    pre_gate = dot_nt(conv_act, conv_gate_w) + c_b_in[1]
    logistic = jax.nn.sigmoid(pre_gate)
    gated = pre_value * logistic * visible

    up = [(i, i + 1) for i in range(mp - 1) if (i + 1) % group]
    down = [(i + 1, i) for i, _ in up]

    halo = -(-reach // 8) * 8

    def halos(rows):
        return lax.ppermute(rows[-halo:], "mp", up), lax.ppermute(rows[:halo], "mp", down)

    gated_halos = halos(gated)
    depth, stats = depth_forward(gated, gated_halos, c_depth, visible, taps)
    depth, stats, *cot_halves = hold((depth, stats, *cot_halves))
    cot_rows = join_halves(*cot_halves)

    def join(one, two):
        both = jnp.maximum(one[0:1] + two[0:1], 1.0)
        gap = one[1:2] - two[1:2]
        return jnp.concatenate(
            [
                one[0:1] + two[0:1],
                (one[0:1] * one[1:2] + two[0:1] * two[1:2]) / both,
                one[2:3] + two[2:3] + gap * gap * (one[0:1] * two[0:1] / both),
                one[3:],
            ],
            axis=0,
        )

    beside = [None, None, None, None, late_own]
    stats = combine_everywhere(stats, join, beside)
    late_own = beside[4].reshape(2, -1, width)
    late_other = swap(late_own, "mp", 1)
    blocks_b = [(late_own[0], late_own[1], bias_b[0]), (late_other[0], late_other[1], bias_b[1])]
    batch_mean = stats[1:2]
    batch_var = stats[2:3] / valid_count
    inv_batch = lax.rsqrt(batch_var + EPS)
    centred = depth - batch_mean
    normed_bn = centred * inv_batch * c_scale + c_shift
    swished = jax.nn.silu(normed_bn).astype(BF)
    resid_d = resid_c + (dot_nn(swished, conv_out_w) + conv_b_out)

    branch, saved_b = ffn_forward(resid_d, ffb_gain, ffb_shift, blocks_b, ffb_b_out)
    resid_e = resid_d + 0.5 * branch
    layer_rows, unit_out, inv_out = norm_forward(resid_e, final_gain, final_shift)

    grad_resid, g_final_gain, g_final_shift = norm_backward(
        cot_rows.astype(F32), unit_out, inv_out, final_gain
    )
    grad_resid, mats_b, vecs_b = ffn_backward(grad_resid, saved_b, ffb_gain, blocks_b)

    def by_core(rows):
        part = width // 2
        return [
            lax.dynamic_slice_in_dim(rows, which * part, part, axis=1) for which in (core, 1 - core)
        ]

    grad_branch = grad_resid.astype(BF)
    g_conv_b_out = jnp.sum(grad_branch, axis=0, dtype=F32, keepdims=True)
    grad_normed = dot_nt(grad_branch, conv_out_w) * swish_slope(normed_bn)
    g_conv_out = [dot_tn(rows, grad_branch).astype(BF) for rows in by_core(swished)]
    sums = jnp.concatenate(
        [
            jnp.sum(grad_normed, axis=0, keepdims=True),
            jnp.sum(grad_normed * centred, axis=0, keepdims=True),
        ],
        axis=0,
    )
    late_g = [mats_b[0][1], mats_b[2][1], mats_b[0][0], mats_b[2][0]]
    sums = combine_everywhere(sums, jnp.add, late_g)
    late_got = [swap(grads, "mp", 1) for grads in late_g[:2]]
    sums, layer_rows = hold((sums, layer_rows.astype(BF)))
    layer_out = send_back(layer_rows)
    grad_normed, *late_got = hold((grad_normed, *late_got))
    late_sum = add_parts(late_g[2], late_got[0], late_g[3], late_got[1], 1)
    late_sum = late_sum.reshape(2 * zs, dp * hidden_q, width)
    late_sum = lax.psum_scatter(late_sum, "dp", scatter_dimension=1, tiled=True)
    inv_cube = inv_batch * inv_batch * inv_batch
    grad_depth = grad_normed * (c_scale * inv_batch) - visible * (
        (inv_batch * c_scale * sums[0:1] + inv_cube * c_scale * sums[1:2] * centred) / valid_count
    )
    grad_value_pre, grad_gate_pre, g_depth, g_conv_b_in = depth_backward(
        grad_depth,
        halos(grad_depth),
        gated,
        gated_halos,
        c_depth,
        visible,
        pre_value,
        logistic,
        taps,
    )
    grad_act = dot_nn(grad_value_pre, conv_value_w) + dot_nn(grad_gate_pre, conv_gate_w)
    g_conv_value = [dot_tn(rows, conv_act).astype(BF) for rows in by_core(grad_value_pre)]
    g_conv_gate = [dot_tn(rows, conv_act).astype(BF) for rows in by_core(grad_gate_pre)]
    grad_in, g_conv_gain, g_conv_shift = norm_backward(grad_act, conv_unit, conv_inv, conv_gain)
    grad_resid = grad_resid + grad_in

    grad_branch = grad_resid.astype(BF)
    g_att_b_out = jnp.sum(grad_branch, axis=0, dtype=F32, keepdims=True)
    grad_mixed = dot_nt(grad_branch, att_out_w).astype(BF)
    g_att_out = []
    for which in range(2):
        one = [
            lax.dynamic_slice_in_dim(
                mixed,
                ((((q // 2) ^ k) * 2 + which) * 2 + slot) * columns,
                columns,
                axis=1,
            )
            for slot in range(2)
            for k in range(group // 2)
        ]
        g_att_out.append(dot_tn(jnp.concatenate(one, axis=1), grad_branch).astype(BF))
    wide = 2 * columns
    parts = [grad_mixed[:, r * wide : (r + 1) * wide] for r in range(group)]
    grad_cols = jnp.concatenate(exchange_blocks(parts), axis=0)
    grad_q, grad_k, grad_v = attend_backward(
        query, key, value, grad_cols, mixed_wide, lse, key_bias, block
    )

    grad_q, grad_k, grad_v, late_sum = hold((grad_q, grad_k, grad_v, late_sum))
    late_sum = late_sum.reshape(2, zs, hidden_q, width)
    late_parts = reordered(jnp.moveaxis(late_sum, 1, 0).reshape(zs, -1, width), m // 2)
    if rounds_fit():
        late_got = swap(late_parts[1::2], "mp", 2)
    mid_g = [g_conv_value, g_conv_gate, g_conv_out, g_att_out]
    mid_got = swap(jnp.concatenate([g[1] for g in mid_g], axis=0), "mp", 1)
    grad_all = jnp.concatenate([grad_q, grad_k, grad_v], axis=1)
    w_flat = jnp.concatenate([w_qkv[0], w_qkv[1], w_qkv[2]], axis=1)
    partial = dot_nt(grad_all, w_flat)
    g_qkv = dot_tn(grad_all, att_rows).astype(BF)
    partial, *layer_out = hold((partial, *layer_out))
    partial = [partial[r * rows_local : (r + 1) * rows_local] for r in range(group)]
    if rounds_fit():
        got_0, got_1, mid_got = hold(
            (
                swap(partial[1].astype(BF), "mp", 1),
                swap(partial[3].astype(BF), "mp", 1),
                mid_got,
            )
        )
        to_near = (partial[2] + got_1.astype(F32)).astype(BF)
        to_near, mid_got, g_qkv = hold((to_near, mid_got, g_qkv))
    mid_got = mid_got.reshape(4, zs, columns, width)
    joint = [
        add_rounded(g[0].reshape(zs, columns, width), got)
        for g, got in zip(mid_g, mid_got, strict=True)
    ] + [g_qkv.reshape(6, columns, width)]
    joint_rows = (4 * zs + 6) * chan_q
    if rounds_fit():
        joint_parts = []
        for r in range(dp):
            part = [
                lax.dynamic_slice_in_dim(rows, (d ^ r) * chan_q, chan_q, axis=1) for rows in joint
            ]
            joint_parts.append(jnp.concatenate(part, axis=0).reshape(joint_rows, width))
        joint_corners = corners(joint_parts)
    if rounds_fit():
        got, late_got, *joint_corners = hold((swap(to_near, "mp", 2), late_got, *joint_corners))
        grad_act = partial[0] + got_0.astype(F32) + got.astype(F32)
        joint_sides = sides(joint_parts, *joint_corners)
        late_parts = add_rounded(late_parts[0::2], late_got)
    else:
        grad_act = collect_blocks(partial)
    g_qv = jnp.stack(
        [jnp.sum(grad_q, axis=0, dtype=F32), jnp.sum(grad_v, axis=0, dtype=F32)]
    ).reshape(2, 2, 1, columns)
    g_b_qv = lax.dynamic_update_slice(
        jnp.zeros((2, 2, group, columns), F32), g_qv, (0, 0, q, 0)
    ).reshape(2, width)
    grad_in, g_att_gain, g_att_shift = norm_backward(grad_act, att_unit, att_inv, att_gain)
    grad_resid = grad_resid + grad_in

    def joint_pieces(rows):
        rows = rows.reshape(-1, chan_q, width)
        parts = jnp.moveaxis(rows[: 4 * zs].reshape(4, zs, chan_q, width), 1, 0)
        parts = reordered(parts.reshape(zs, -1, width), m // 2)
        pair = rows[4 * zs :].reshape(3, 2, chan_q, width)
        pair = [
            lax.dynamic_index_in_dim(pair, which, 1, keepdims=False).reshape(-1, width)
            for which in (half, 1 - half)
        ]
        return parts, pair

    flight = {}

    def between(step, held):
        kind, k = step
        if kind == "rest":
            held, flight["a_parts"] = hold((held, flight["a_parts"]))
            flight["corners"] = corners(flight["a_parts"])
        elif kind == "upper":
            if k == 0:
                held, mid_got = hold((held, flight["mid_got"]))
                mid = add_rounded(flight["mid"][0::2], mid_got)
                far = swap(jnp.concatenate([mid[1], flight["pair"][1]], axis=0), "mp", 4)
                flight["mid"] = jnp.concatenate([mid[0], flight["pair"][0]], axis=0), far
        elif k == 3:
            held = hold(held)
            flight["b"] = [swap(held[1], "mp", 1), swap(held[2], "mp", 1)]
            flight["late"] = swap(late_parts[1], "mp", 4)
        elif k == 2:
            *held, b_in, b_out = hold((*held, *flight["b"]))
            parts = add_parts(held[1], b_in, held[2], b_out, 4)
            flight["b_parts"] = [parts[r].reshape(-1, width) for r in range(4)]
            flight["corners"] = corners(flight["b_parts"])
        elif k == 1:
            *held, side_x, side_y, to_x, to_y, late_far = hold(
                (*held, *joint_sides, *flight["corners"], flight["late"])
            )
            flight["late"] = add_rounded(late_parts[0], late_far)
            b_sides = sides(flight["b_parts"], to_x, to_y)
            flight["mid"], flight["pair"] = joint_pieces(finish(joint_parts, side_x, side_y))
            flight["mid_got"] = swap(flight["mid"][1::2], "mp", 2)
            a_got = [swap(held[1], "mp", 1), swap(held[2], "mp", 1)]
            flight["k1"] = (*a_got, *b_sides)
        else:
            *held, a_in, a_out, b_x, b_y = hold((*held, *flight["k1"]))
            parts = add_parts(held[1], a_in, held[2], a_out, 4)
            flight["a_parts"] = [parts[r].reshape(-1, width) for r in range(4)]
            b_sum = finish(flight["b_parts"], b_x, b_y).reshape(2, 2, hidden_q, width)
            flight["b_sum"] = b_sum[:, 0], swap(b_sum[:, 1], "mp", 2)
        return held

    grad_resid, mats_a, vecs_a = ffn_backward(
        grad_resid, saved_a, ffa_gain, blocks_a, between if rounds_fit() else None
    )
    g_embed = jnp.sum(grad_resid * flag_rows, axis=0, keepdims=True)
    back_first, back_second = send_back_parts(grad_resid.astype(BF))

    def hidden_order(parts):
        own, other = parts
        both = jnp.stack([jnp.where(core == 0, own, other), jnp.where(core == 0, other, own)])
        return both.reshape(2, zs, dp * hidden_q).transpose(1, 0, 2).reshape(-1, width)

    def relative_order(parts):
        rel = jnp.stack(parts).reshape(2, 2, dp, low, hidden_q)
        rel = rel.transpose(0, 3, 1, 2, 4).reshape(mp, dp, hidden_q)
        return rel[jnp.arange(mp) ^ m][:, jnp.arange(dp) ^ d].reshape(-1, width)

    small = (
        jnp.concatenate(
            [
                from_canon(jnp.concatenate([g_depth[:taps], g_conv_b_in[:2]], axis=0)),
                hidden_order(mats_b[1]),
                relative_order(mats_a[1]),
                g_b_qv,
                *vecs_b,
                g_final_gain,
                g_final_shift,
                g_conv_b_out,
                g_conv_gain,
                g_conv_shift,
                *vecs_a,
                g_embed,
                g_att_b_out,
                g_att_gain,
                g_att_shift,
            ],
            axis=0,
        )
    )
    if rounds_fit():
        b_own, b_near = flight["b_sum"]
        rest, far = flight["mid"]
        to_x, to_y, b_near, far, got = hold(
            (*flight["corners"], b_near, far, swap(small, "dp", 1))
        )
        small = small + got
        side_x, side_y = sides(flight["a_parts"], to_x, to_y)
        rest = jnp.concatenate([flight["late"], add_rounded(rest, far)], axis=0)
        side_x, side_y, b_far, got, rest, back_first, back_second = hold(
            (
                side_x,
                side_y,
                swap(add_rounded(b_own, b_near), "mp", 4),
                swap(small, "dp", 2),
                rest,
                back_first,
                back_second,
            )
        )
        small = small + got
        small = small + swap(small, "mp", 1)
        a_sum = finish(flight["a_parts"], side_x, side_y).reshape(2, 2, hidden_q, width)
        a_near, rest_x, rest_y, got = hold(
            (
                swap(a_sum[:, 1], "mp", 2),
                swap(rest, "dp", 1),
                swap(rest, "dp", 2),
                swap(small, "mp", 2),
            )
        )
        small = small + got
        small, back_first = hold((small + swap(small, "mp", 4), back_first))
        own = a_sum[:, 0].astype(F32) + a_near.astype(F32) + b_far.astype(F32)
        own = own.astype(BF).reshape(-1, width)
        cut = rest.shape[0] // 2
        by_x, by_y, rest_0, rest_1, back_first, back_second = hold(
            (
                swap(own, "dp", 1),
                swap(own, "dp", 2),
                swap(rest_y[:cut], "dp", 1),
                swap(rest_x[cut:], "dp", 2),
                send_straight(back_first),
                back_second,
            )
        )
        back_second = send_crossed(back_second)
        corner = [swap(by_y[:hidden_q], "dp", 1), swap(by_x[hidden_q:], "dp", 2)]
        first = [own, by_x, by_y, corner]
        late_all = [rest, rest_x, rest_y, jnp.concatenate([rest_0, rest_1], axis=0)]
        rest = jnp.stack([part[2 * hidden_q :] for part in late_all])
    else:
        joint = jnp.concatenate(joint, axis=0)
        joint = lax.psum_scatter(joint, "dp", scatter_dimension=1, tiled=True)
        mid_parts, pair = joint_pieces(joint)
        total = collect_plain(
            mats_a[0], mats_a[2], jnp.concatenate([late_parts, mid_parts], axis=1), pair
        )
        back_first, back_second = send_straight(back_first), send_crossed(back_second)
        first, late_all, rest = jnp.split(total, [2 * hidden_q, 4 * hidden_q], axis=1)
        if hidden_q % 128 == 0:
            first = [*first[:-1], [first[-1]]]
        small = combine_everywhere(small, jnp.add)
    if hidden_q % 128 == 0:
        g_ffb_in, g_ffb_out = unpack(list(late_all), d, hidden_q)
    else:
        pairs = []
        for part in (first, late_all):
            part = reordered(part, d).reshape(dp, 2, hidden_q, width).astype(F32)
            part = jnp.moveaxis(part, 1, 0).reshape(2, -1, width)
            pairs += [part[0].T, part[1]]
        g_ffa_in, g_ffa_out, g_ffb_in, g_ffb_out = pairs
    rest = reordered(rest, d).reshape(dp, 7, chan_q, width)
    rest = jnp.moveaxis(rest, 1, 0).reshape(7, columns, width).astype(F32)
    mid_total = rest[:4]
    g_att_qkv = rest[4:].transpose(0, 2, 1)
    g_conv_w_in = jnp.stack([mid_total[0].T, mid_total[1].T])
    if hidden_q % 128 == 0:
        *last, g_ffb_in, g_ffb_out, mid_total, g_att_qkv, g_conv_w_in = hold(
            (*first[3], g_ffb_in, g_ffb_out, mid_total, g_att_qkv, g_conv_w_in)
        )
        first = [*first[:3], jnp.concatenate(last, axis=0)]
        g_ffa_in, g_ffa_out = unpack(first, d, hidden_q)

    total = small
    g_w_depth = own_columns(total[:taps])
    g_b_conv = own_columns(total[taps : taps + 2])
    at = taps + 2
    hidden_rows = mp * hidden_q * dp // width
    share = mats_b[1][0].shape[1] * 2 // mp

    def own_hidden(rows):
        return lax.dynamic_slice_in_dim(rows.reshape(-1), m * share, share, axis=0)

    g_ffb_b_in = own_hidden(total[at : at + hidden_rows])
    g_ffa_b_in = own_hidden(total[at + hidden_rows : at + 2 * hidden_rows])
    at = at + 2 * hidden_rows
    g_qv_out = own_columns(total[at : at + 2])
    e = total[at + 2 :]
    f = e[8:]

    def own_canon(vector):
        return own_columns(from_canon(vector))[0]

    mean_own = own_canon(batch_mean)
    var_own = own_canon(batch_var)
    g_scale = own_canon(sums[1:2] * inv_batch)
    g_shift = own_canon(sums[0:1])
    new_mean = 0.9 * running_mean + 0.1 * mean_own
    new_var = 0.9 * running_var + 0.1 * var_own * valid_count / (valid_count - 1.0)
    return (
        join_back(*layer_out),
        join_back(back_first, back_second),
        f[3],
        f[0],
        f[1],
        g_ffa_in,
        g_ffa_b_in,
        g_ffa_out,
        f[2],
        f[5],
        f[6],
        g_att_qkv,
        g_qv_out,
        mid_total[3],
        f[4],
        e[6],
        e[7],
        g_conv_w_in,
        g_b_conv,
        g_w_depth,
        g_scale,
        g_shift,
        mid_total[2],
        e[5],
        e[0],
        e[1],
        g_ffb_in,
        g_ffb_b_in,
        g_ffb_out,
        e[2],
        e[3],
        e[4],
        new_mean,
        new_var,
    )


def solution(mesh):
    return jax.shard_map(
        shards,
        mesh=mesh,
        in_specs=(
            P("dp", "mp", None),
            P("dp"),
            P("dp", "mp"),
            P(),
            P(),
            P(),
            P(None, "mp"),
            P("mp"),
            P("mp", None),
            P(),
            P(),
            P(),
            P(None, None, "mp"),
            P(None, "mp"),
            P("mp", None),
            P(),
            P(),
            P(),
            P(None, None, "mp"),
            P(None, "mp"),
            P(None, "mp"),
            P("mp"),
            P("mp"),
            P("mp"),
            P("mp"),
            P("mp", None),
            P(),
            P(),
            P(),
            P(None, "mp"),
            P("mp"),
            P("mp", None),
            P(),
            P(),
            P(),
            P("dp", "mp", None),
        ),
        out_specs=(
            P("dp", "mp", None),
            P("dp", "mp", None),
            P(),
            P(),
            P(),
            P(None, "mp"),
            P("mp"),
            P("mp", None),
            P(),
            P(),
            P(),
            P(None, None, "mp"),
            P(None, "mp"),
            P("mp", None),
            P(),
            P(),
            P(),
            P(None, None, "mp"),
            P(None, "mp"),
            P(None, "mp"),
            P("mp"),
            P("mp"),
            P("mp", None),
            P(),
            P(),
            P(),
            P(None, "mp"),
            P("mp"),
            P("mp", None),
            P(),
            P(),
            P(),
            P("mp"),
            P("mp"),
        ),
        check_vma=False,
    )
```
